256 devices in a mesh: seq: 16 (over x_lo, z), tp: 16 (over y, x_hi, core).
Axes of the slice: x: 4 (x_hi: 2, x_lo: 2; x = x_hi * 2 + x_lo), y: 4, z: 8, core: 2. Of those that a mesh axis runs over, the one named last changes fastest.
Arguments:
- inputs: bfloat16 [32768, 1536], P('seq', 'tp'), may hold values from -6 to 6
- grad_out: bfloat16 [32768, 1536], P('seq', 'tp'), may hold values from -6 to 6
- kernel: float32 [15, 1536], P(None, 'tp'), may hold values from -2 to 2
- ln_gain: float32 [1536], replicated, may hold values from 0.4 to 2.5
- layer_scale: float32 [1536], replicated, may hold values from 0.2 to 2
- w_up: bfloat16 [1536, 6144], P(None, 'tp'), may hold values from -0.15625 to 0.15625
- w_down: bfloat16 [6144, 1536], P('tp'), may hold values from -0.078125 to 0.078125
Outputs:
- grad_inputs: bfloat16 [32768, 1536], P('seq', 'tp')
- grad_up: float32 [1536, 6144], P('seq', 'tp')
- grad_down_t: float32 [1536, 6144], P('seq', 'tp')
- grad_kernel: float32 [15, 1536], P(None, 'tp')
The draws below stay inside these ranges and needn't reach their ends.
All inputs are finite; a program needn't handle non-finite values.
Results may differ from the reference program's by a relative error of at most 0.023.
Values may be sent and summed in bfloat16 or wider, within the bound.
A program may use at most 128 MiB of HBM per device.

```python
import math
import jax
import jax.numpy as jnp
from jax import lax

D = 1536
FF = 6144
KW = 15
TOK_DEV = 2048
SEQ_LEN = 32768
N_TP = 16


def draw_kernel(key, part):
    key = jax.random.fold_in(key, 11)
    key_base, key_jitter = jax.random.split(key)
    channel = jnp.arange(D, dtype=jnp.float32) / (D - 1)
    trend = jnp.exp(jnp.log(0.55) + channel * jnp.log(1.8 / 0.55))
    jitter = jnp.exp(jax.random.uniform(key_jitter, (D,), jnp.float32, jnp.log(0.7), jnp.log(1.4)))
    base = jnp.clip(jax.random.normal(key_base, (KW, D), jnp.float32), -3.0, 3.0)
    return jnp.clip(base * trend * jitter / jnp.sqrt(jnp.float32(KW)), -2.0, 2.0)


def block_scale(stream_key, shape, pieces, low, high):
    level = 1.0
    for position, blocks in pieces:
        draws = jax.random.uniform(jax.random.fold_in(jax.random.fold_in(stream_key, 6), position), (blocks,), jnp.float32, low / len(pieces), high / len(pieces))
        level = level * jnp.repeat(jnp.exp(draws), shape[position] // blocks).reshape((-1,) + (1,) * (len(shape) - 1 - position))
    return level


def normal_values(rng, extent, deviation, limit, pieces=(), held_as=jnp.bfloat16):
    array = deviation * jax.random.normal(rng, extent, jnp.float32)
    if pieces:
        array = array * block_scale(rng, extent, pieces, -0.22, 0.18)
    return jnp.clip(array, -limit, limit).astype(held_as)


def setup_inputs(seed: int = 0) -> dict:
    key_of = jax.random.split(jax.random.key(seed), 8)
    inputs = normal_values(key_of[0], (SEQ_LEN, D), 1.0, 6.0, ((0, 16), (1, 16)))
    grad_out = normal_values(key_of[1], (SEQ_LEN, D), 1.0, 6.0, ((0, 16), (1, 16)))
    kernel = draw_kernel(jax.random.fold_in(key_of[7], 71), 0)
    ln_gain = jnp.clip(jnp.exp(jax.random.uniform(key_of[3], (D,), jnp.float32, math.log(0.4), math.log(2.5))), 0.4, 2.5)
    layer_scale = jnp.clip(jnp.exp(jax.random.uniform(key_of[4], (D,), jnp.float32, math.log(0.2), math.log(2.0))), 0.2, 2.0)
    w_up = normal_values(key_of[5], (D, FF), D ** -0.5, 0.15625, ((1, 16),))
    w_down = normal_values(key_of[6], (FF, D), FF ** -0.5, 0.078125, ((0, 16),))
    return dict(inputs=inputs, grad_out=grad_out, kernel=kernel, ln_gain=ln_gain, layer_scale=layer_scale, w_up=w_up, w_down=w_down)


def gelu_value(pre):
    return 0.5 * pre * (1.0 + lax.erf(pre * 0.7071067811865476))

def gelu_slope(pre):
    return 0.5 * (1.0 + lax.erf(pre * 0.7071067811865476)) + pre * jnp.exp(-0.5 * pre * pre) * 0.3989422804014327

def reference(inputs, grad_out, kernel, ln_gain, layer_scale, w_up, w_down):
    reach = KW // 2
    values = inputs.astype(jnp.float32)
    padded = jnp.pad(values, ((reach, reach), (0, 0)))
    conv = sum((kernel[offset] * padded[offset:offset + SEQ_LEN] for offset in range(KW)))
    row_mean = lax.optimization_barrier(jnp.mean(conv, axis=1, keepdims=True))
    row_var = lax.optimization_barrier(jnp.mean(conv * conv, axis=1, keepdims=True)) - row_mean * row_mean
    rstd = lax.rsqrt(row_var + 1e-06)
    nhat = (conv - row_mean) * rstd
    normed = (nhat * ln_gain).astype(jnp.bfloat16)
    scaled = (layer_scale * grad_out.astype(jnp.float32)).astype(jnp.bfloat16)
    group_width = FF // N_TP
    blocks = SEQ_LEN // TOK_DEV
    up_groups = w_up.reshape(D, N_TP, group_width).astype(jnp.float32)

    def block_step(carry, pair):
        normed_blk, scaled_blk = pair
        pre_act = jnp.dot(normed_blk, w_up, preferred_element_type=jnp.float32)
        hidden = gelu_value(pre_act).astype(jnp.bfloat16)
        grad_hidden = jnp.dot(scaled_blk, w_down.T, preferred_element_type=jnp.float32)
        grad_pre = (grad_hidden * gelu_slope(pre_act)).astype(jnp.bfloat16)
        acc_up = carry[0] + jnp.dot(normed_blk.T, grad_pre, preferred_element_type=jnp.float32)
        acc_down = carry[1] + jnp.dot(scaled_blk.T, hidden, preferred_element_type=jnp.float32)
        partials = jnp.einsum('bgf,cgf->gbc', grad_pre.reshape(TOK_DEV, N_TP, group_width).astype(jnp.float32), up_groups)
        rounded = lax.optimization_barrier(partials.astype(jnp.bfloat16))
        grad_normed = lax.optimization_barrier(jnp.sum(rounded.astype(jnp.float32), axis=0))
        return ((acc_up, acc_down), grad_normed)
    start = (jnp.zeros((D, FF), jnp.float32), jnp.zeros((D, FF), jnp.float32))
    (acc_up, acc_down), grad_blocks = lax.scan(block_step, start, (normed.reshape(blocks, TOK_DEV, D), scaled.reshape(blocks, TOK_DEV, D)))
    grad_normed = grad_blocks.reshape(SEQ_LEN, D)
    scaled_g = grad_normed * ln_gain
    first_mean = lax.optimization_barrier(jnp.mean(scaled_g, axis=1, keepdims=True))
    second_mean = lax.optimization_barrier(jnp.mean(scaled_g * nhat, axis=1, keepdims=True))
    grad_conv = rstd * (scaled_g - first_mean - nhat * second_mean)
    grad_pad = jnp.pad(grad_conv, ((reach, reach), (0, 0)))
    grad_inputs = grad_out.astype(jnp.float32) + sum((kernel[offset] * grad_pad[2 * reach - offset:2 * reach - offset + SEQ_LEN] for offset in range(KW)))
    factor = lax.rsqrt(jnp.asarray(SEQ_LEN, jnp.float32))
    grad_kernel = jnp.stack([lax.optimization_barrier(jnp.sum(grad_conv * padded[offset:offset + SEQ_LEN], axis=0)) for offset in range(KW)]) * factor
    return (grad_inputs.astype(jnp.bfloat16), acc_up * factor, acc_down * factor, grad_kernel)
```

```python
import functools
import math

import jax
import jax.numpy as jnp
from jax import lax
from jax.experimental import pallas as pl
from jax.experimental.pallas import tpu as pltpu
from jax.sharding import PartitionSpec as P

MESH = pl.DeviceIdType.MESH
BF = jnp.bfloat16
F32 = jnp.float32

TP = 16
NY = 4
SEQ = 16
NZ = 8
W = 96
D = 1536
TOK = 2048
HALF = TOK // 2
NC = 4
TC = HALF // NC
U = 384
KW = 15
REACH = KW // 2
PAD = 128


def nn(a, b):
    return jnp.dot(a, b, preferred_element_type=F32)


def nt(a, b):
    return lax.dot_general(a, b, (((1,), (1,)), ((), ())), preferred_element_type=F32)


def shifted(x, by):
    width = x.shape[1]
    return pltpu.roll(x, (-by) % width, 1) if by else x


def body(
    x_t, go_t, taps, gain_l, scale_l, gain_all, wu, wu_t, wd,
    gi_t, gu, gd, gk,
    s_st, n_st, g_s, g_n, xp, cv, hin, st_s, st_r, mr, wu_p, wu_tp, wd_p, pre_s, gh_s,
    hid, gpr, pf, s1, r1, s2, r2, s3, r3, own, bst, bst_r, gc, gch_s, gch, gkp, gks, gkr,
    wf, c_s, c_r, z_s, z_r, x_s, x_r,
    halo_ss, halo_rs, w_ss, w_rs, st_ss, st_rs, a1_ss, a1_rs, a2_ss, a2_rs, a3_ss, a3_rs,
    r1_ss, r1_rs, r2_ss, r2_rs, r3_ss, r3_rs, b_ss, b_rs, gh_ss, gh_rs, gk_ss, gk_rs,
    c_ss, c_rs, z_ss, z_rs, x_ss, x_rs,
):
    tp = lax.axis_index("tp")
    sq = lax.axis_index("seq")
    k = lax.rem(tp, 2)
    xh = lax.rem(tp // 2, 2)
    y = tp // 4
    xl = sq // NZ
    z = lax.rem(sq, NZ)

    def at(y_, xh_, k_):
        return {"seq": sq, "tp": (y_ * 2 + xh_) * 2 + k_}

    def send(src, dst, ss, rs, dev):
        return pltpu.make_async_remote_copy(
            src_ref=src, dst_ref=dst, send_sem=ss, recv_sem=rs, device_id=dev, device_id_type=MESH
        )

    up, down = lax.rem(y + 1, NY), lax.rem(y + NY - 1, NY)
    anti = lax.rem(y + 2, NY)
    y_dev = (at(up, xh, k), at(down, xh, k))
    other = 1 - k
    near = (at(y, 1 - xh, k), at(y, xh, other), at(y, 1 - xh, other))
    sq_next, sq_prev = lax.rem(sq + 1, SEQ), lax.rem(sq + SEQ - 1, SEQ)
    sq_dev = ({"seq": sq_next, "tp": tp}, {"seq": sq_prev, "tp": tp})
    z_dev = (
        {"seq": xl * NZ + lax.rem(z + 1, NZ), "tp": tp},
        {"seq": xl * NZ + lax.rem(z + NZ - 1, NZ), "tp": tp},
    )
    x_dev = {"seq": (1 - xl) * NZ + z, "tp": tp}
    my_rows = pl.ds(pl.multiple_of(tp * W, 32), W)

    def y_rows(which, first=0, count=4 * W):
        return pl.ds(pl.multiple_of(which * (4 * W) + first, 32), count)

    barrier = pltpu.get_barrier_semaphore()
    for j in range(1, TP):
        pl.semaphore_signal(
            barrier, inc=1, device_id={"seq": sq, "tp": lax.rem(tp + j, TP)}, device_id_type=MESH
        )
    for j in range(1, SEQ):
        pl.semaphore_signal(
            barrier, inc=1, device_id={"seq": lax.rem(sq + j, SEQ), "tp": tp}, device_id_type=MESH
        )
    pl.semaphore_wait(barrier, TP + SEQ - 2)

    def halo(d):
        src = x_t.at[:, pl.ds(TOK - PAD, PAD)] if d == 0 else x_t.at[:, pl.ds(0, PAD)]
        return send(src, hin.at[d], halo_ss.at[d], halo_rs.at[d], sq_dev[d])

    def weight(i):
        src, dst = ((wd, wd_p), (wu_t, wu_tp), (wu, wu_p))[i]
        return send(src, dst, w_ss.at[i], w_rs.at[i], near[1])

    def stat_out(j):
        return send(
            st_s, st_r.at[tp], st_ss.at[j], st_rs.at[tp], {"seq": sq, "tp": lax.rem(tp + j, TP)}
        )

    def stat_in(j):
        src = lax.rem(tp + j, TP)
        return send(st_s, st_r.at[src], st_ss.at[j], st_rs.at[src], {"seq": sq, "tp": src})

    staged, full = (s_st, n_st), (g_s, g_n)

    def ag1(a, c, j):
        src = staged[a].at[k if j == 0 else other, c]
        i = (a * NC + c) * 3 + j
        return send(src, full[a].at[c, my_rows], a1_ss.at[i], a1_rs.at[i], near[j])

    def ag2(a, c, d):
        part = full[a].at[c, y_rows(y)]
        i = (a * NC + c) * 2 + d
        return send(part, part, a2_ss.at[i], a2_rs.at[i], y_dev[d])

    def ag3(a, c, d):
        part = full[a].at[c, y_rows(down, 0, 2 * W) if d == 0 else y_rows(up, 2 * W, 2 * W)]
        i = (a * NC + c) * 2 + d
        return send(part, part, a3_ss.at[i], a3_rs.at[i], y_dev[d])

    def rs1(c, d):
        i = c * 2 + d
        return send(s1.at[d, c], r1.at[d, c], r1_ss.at[i], r1_rs.at[i], y_dev[d])

    def rs2(c, d):
        i = c * 2 + d
        return send(s2.at[d, c], r2.at[d, c], r2_ss.at[i], r2_rs.at[i], y_dev[d])

    def rs3(c, j):
        i = c * 3 + j
        return send(s3.at[c, j], r3.at[c, j], r3_ss.at[i], r3_rs.at[i], near[j])

    def bstat_out(j):
        return send(
            bst, bst_r.at[tp], b_ss.at[j], b_rs.at[tp], {"seq": sq, "tp": lax.rem(tp + j, TP)}
        )

    def bstat_in(j):
        src = lax.rem(tp + j, TP)
        return send(bst, bst_r.at[src], b_ss.at[j], b_rs.at[src], {"seq": sq, "tp": src})

    def ghalo(d):
        return send(gch_s.at[d], gch.at[d], gh_ss.at[d], gh_rs.at[d], sq_dev[d])

    def gk_out(j):
        return send(
            gks, gkr.at[sq], gk_ss.at[j], gk_rs.at[sq], {"seq": lax.rem(sq + j, SEQ), "tp": tp}
        )

    def gk_in(j):
        src = lax.rem(sq + j, SEQ)
        return send(gks, gkr.at[src], gk_ss.at[j], gk_rs.at[src], {"seq": src, "tp": tp})

    def core_w(i):
        return send(c_s.at[i], c_r.at[i], c_ss.at[i], c_rs.at[i], near[1])

    def ring(d, step, e):
        i = (d * 4 + step) * 2 + e
        if step == 0:
            return send(
                z_s.at[d, step, e, pl.ds(d, 1)], z_r.at[d, step, e, pl.ds(d, 1)],
                z_ss.at[i], z_rs.at[i], z_dev[d],
            )
        return send(z_s.at[d, step, e], z_r.at[d, step, e], z_ss.at[i], z_rs.at[i], z_dev[d])

    def x_swap():
        return send(x_s, x_r, x_ss.at[0], x_rs.at[0], x_dev)

    for d in range(2):
        halo(d).start()
    for c in range(NC):
        for h in range(2):
            cols = pl.ds(h * HALF + c * TC, TC)
            s_st[h, c] = (scale_l[...] * go_t[:, cols].astype(F32)).astype(BF)
        for j in (2, 0, 1):
            ag1(0, c, j).start()
        g_s[c, my_rows] = s_st[k, c]
    for i in range(3):
        weight(i).start()

    xp[:, pl.ds(PAD, TOK)] = x_t[...].astype(F32)
    for d in range(2):
        halo(d).wait_recv()
    xp[:, pl.ds(0, PAD)] = jnp.where(sq == 0, 0.0, hin[0].astype(F32))
    xp[:, pl.ds(PAD + TOK, PAD)] = jnp.where(sq == SEQ - 1, 0.0, hin[1].astype(F32))

    def conv_rows(i, sums):
        rows = pl.ds(pl.multiple_of(i * 8, 8), 8)
        x = xp[rows, :]
        t = taps[rows, :]
        total = None
        for tap in range(KW):
            term = t[:, tap : tap + 1] * shifted(x, tap - REACH)[:, PAD : PAD + TOK]
            total = term if total is None else total + term
        cv[rows, :] = total
        return sums[0] + total, sums[1] + total * total

    zero = jnp.zeros((8, TOK), F32)
    first, second = lax.fori_loop(0, W // 8, conv_rows, (zero, zero))
    st_s[0:1, :] = jnp.sum(first, axis=0, keepdims=True)
    st_s[1:2, :] = jnp.sum(second, axis=0, keepdims=True)
    for j in range(1, TP):
        stat_out(j).start()
    st_r[tp] = st_s[...]

    def pass_on_1(a, c):
        for j in range(3):
            ag1(a, c, j).wait_recv()
        for d in range(2):
            ag2(a, c, d).start()

    def pass_on_2(a, c):
        for d in range(2):
            ag2(a, c, d).wait_recv()
            ag3(a, c, d).start()

    pass_on_1(0, 0)
    for j in range(1, TP):
        stat_in(j).wait_recv()
    totals = st_r[0]
    for j in range(1, TP):
        totals = totals + st_r[j]
    mean = totals[0:1] / D
    var = totals[1:2] / D - mean * mean
    mr[0:1, :] = mean
    mr[1:2, :] = lax.rsqrt(var + 1e-06)
    for c in range(NC):
        for h in range(2):
            cols = pl.ds(h * HALF + c * TC, TC)
            nhat = (cv[:, cols] - mr[0:1, cols]) * mr[1:2, cols]
            n_st[h, c] = (nhat * gain_l[...]).astype(BF)
        for j in (2, 0, 1):
            ag1(1, c, j).start()
        g_n[c, my_rows] = n_st[k, c]

    for c in range(1, NC):
        pass_on_1(0, c)
    for c in range(NC):
        pass_on_2(0, c)
        pass_on_1(1, c)
    for i in range(3):
        weight(i).wait_recv()
    pass_on_2(1, 0)

    def rs2_step(c):
        for d, to in ((0, up), (1, down)):
            rs1(c, d).wait_recv()
            a, b = d * 2 * W, (1 - d) * 2 * W
            got = pf[c, y_rows(to, a, 2 * W)] + r1[d, c].astype(F32)
            s2[d, c, pl.ds(a, 2 * W)] = got.astype(BF)
            s2[d, c, pl.ds(b, 2 * W)] = pf[c, y_rows(to, b, 2 * W)].astype(BF)
            rs2(c, d).start()

    def rs3_step(c):
        for d in range(2):
            rs2(c, d).wait_recv()

        def group(g):
            rows = pl.ds(pl.multiple_of(g * W, 32), W)
            mine = pf[c, y_rows(y, g * W, W)]
            return mine + r2[0, c, rows].astype(F32) + r2[1, c, rows].astype(F32)

        for j, (xh_, k_) in ((2, (1 - xh, other)), (0, (1 - xh, k)), (1, (xh, other))):
            s3[c, j] = group(xh_ * 2 + k_).astype(BF)
            rs3(c, j).start()
        own[c] = group(xh * 2 + k)

    def chunk(c, carry):
        for a in range(2):
            for d in range(2):
                ag3(a, c, d).wait_recv()

        acc = jnp.zeros((8, TC), F32)
        for u, (w_t, w_d) in enumerate(((wu_t, wd), (wu_tp, wd_p))):
            pre_s[...] = nn(w_t[...], g_n[c])
            gh_s[...] = nn(w_d[...], g_s[c])

            def act(i, acc, u=u):
                rows = pl.ds(pl.multiple_of(i * 32, 32), 32)
                v = pre_s[rows, :]
                phi = 0.5 + 0.5 * lax.erf(v * 0.7071067811865476)
                slope = phi + v * jnp.exp(-0.5 * v * v) * 0.3989422804014327
                gp = (gh_s[rows, :] * slope).astype(BF)
                to = pl.ds(pl.multiple_of(u * U + i * 32, 32), 32)
                hid[c, to] = (v * phi).astype(BF)
                gpr[c, to] = gp
                return acc + jnp.sum((gp.astype(F32) * v).reshape(4, 8, TC), axis=0)

            acc = lax.fori_loop(0, U // 32, act, acc)
        second = jnp.sum(acc, axis=0, keepdims=True)

        @pl.when(c < NC - 1)
        def _():
            pass_on_2(1, c + 1)

        acc = jnp.zeros((8, TC), F32)
        for r in range(NY):
            rows = pl.ds(r * 4 * W, 4 * W)
            p = nn(wu[rows, :], gpr[c, pl.ds(0, U)]) + nn(wu_p[rows, :], gpr[c, pl.ds(U, U)])
            pf[c, rows] = p
            acc = acc + jnp.sum((gain_all[rows, :] * p).reshape(4 * W // 8, 8, TC), axis=0)
        cols = pl.ds(pl.multiple_of(c * TC, TC), TC)
        bst[0:1, cols] = jnp.sum(acc, axis=0, keepdims=True)
        bst[1:2, cols] = second
        for d in range(2):
            s1[d, c] = pf[c, y_rows(anti, d * 2 * W, 2 * W)].astype(BF)
            rs1(c, d).start()

        @pl.when(c >= 1)
        def _():
            rs2_step(c - 1)

        @pl.when(c >= 2)
        def _():
            rs3_step(c - 2)

        return carry

    lax.fori_loop(0, NC, chunk, 0)
    for j in range(1, TP):
        bstat_out(j).start()
    bst_r[tp] = bst[...]

    order = (4, 3, 5, 2, 6, 1, 7, 0)

    def block_of(off):
        return lax.rem(z + off, NZ)

    def weight_block(i, carry):
        half = (i + 1) // 2
        off = jnp.where(lax.rem(i, 2) == 1, 4 - half, 4 + half)
        off = lax.rem(off, NZ)
        b = lax.rem(z + off, NZ)
        for e in range(2):
            rows = pl.ds(pl.multiple_of(e * (NZ * W) + b * W, 32), W)
            for a, (left, right) in enumerate(((g_n, gpr), (g_s, hid))):
                total = nt(left[0, rows], right[0])
                for c in range(1, NC):
                    total = total + nt(left[c, rows], right[c])
                wf[b, e, a] = total[:, :U]
                c_s[i, e, a] = total[:, U:].astype(BF)
        core_w(i).start()
        return carry

    def ring_step(i):
        off = order[i]
        b = block_of(off)
        core_w(i).wait_recv()
        if off == 4:
            for e in range(2):
                for d in range(2):
                    got = wf[b, e, d] + c_r[i, e, d].astype(F32)
                    z_s[d, 0, e, d] = got.astype(BF)
                    ring(d, 0, e).start()
        elif off != 0:
            d = 0 if off < 4 else 1
            step = 4 - off if off < 4 else off - 4
            for e in range(2):
                ring(d, step - 1, e).wait_recv()
                for a in range(2):
                    got = wf[b, e, a] + c_r[i, e, a].astype(F32)
                    if step > 1 or a == d:
                        got = got + z_r[d, step - 1, e, a].astype(F32)
                    z_s[d, step, e, a] = got.astype(BF)
                ring(d, step, e).start()
        else:
            for e in range(2):
                for d in range(2):
                    ring(d, 3, e).wait_recv()

            def part(e, a):
                got = wf[b, e, a] + c_r[i, e, a].astype(F32)
                return got + z_r[0, 3, e, a].astype(F32) + z_r[1, 3, e, a].astype(F32)

            for a in range(2):
                x_s[a] = part(1 - xl, a).astype(BF)
            x_swap().start()
            for a in range(2):
                wf[b, xl, a] = part(xl, a)

    lax.fori_loop(0, 3, weight_block, 0)
    rs2_step(NC - 1)
    rs3_step(NC - 2)
    ring_step(0)
    lax.fori_loop(3, NZ, weight_block, 0)
    rs3_step(NC - 1)
    ring_step(1)
    ring_step(2)

    for j in range(1, TP):
        bstat_in(j).wait_recv()
    for c in range(NC):
        for j in range(3):
            rs3(c, j).wait_recv()
    for h in range(2):
        sums = bst_r[h]
        for j in range(1, TP // 2):
            sums = sums + bst_r[2 * j + h]
        m1 = sums[0:1] / D
        m2 = sums[1:2] / D
        for c in range(NC):
            cols = pl.ds(h * HALF + c * TC, TC)
            rel = slice(c * TC, (c + 1) * TC)
            here = own[c] + r3[c, 0].astype(F32)
            there = r3[c, 1].astype(F32) + r3[c, 2].astype(F32)
            scaled_g = jnp.where(k == h, here, there) * gain_l[...]
            rstd = mr[1:2, cols]
            nhat = (cv[:, cols] - mr[0:1, cols]) * rstd
            gc[:, pl.ds(PAD + h * HALF + c * TC, TC)] = rstd * (
                scaled_g - m1[:, rel] - nhat * m2[:, rel]
            )
    gch_s[0] = gc[:, pl.ds(TOK, PAD)]
    gch_s[1] = gc[:, pl.ds(PAD, PAD)]
    for d in range(2):
        ghalo(d).start()

    ring_step(3)
    ring_step(4)

    gkp[...] = jnp.zeros_like(gkp)
    lane = lax.broadcasted_iota(jnp.int32, (8, 128), 1)

    def tap_rows(i, carry):
        rows = pl.ds(pl.multiple_of(i * 8, 8), 8)
        x = xp[rows, :]
        g = gc[rows, pl.ds(PAD, TOK)]
        total = jnp.zeros((8, 128), F32)
        for tap in range(KW):
            prod = g * shifted(x, tap - REACH)[:, PAD : PAD + TOK]
            total = jnp.where(lane == tap, jnp.sum(prod, axis=1, keepdims=True), total)
        gkp[rows, :] = total
        return carry

    lax.fori_loop(0, W // 8, tap_rows, 0)
    gks[...] = gkp[...].T[0:16, :]
    for j in range(1, SEQ):
        gk_out(j).start()
    gkr[sq] = gks[...]

    ring_step(5)
    ring_step(6)

    for d in range(2):
        ghalo(d).wait_recv()
    gc[:, pl.ds(0, PAD)] = jnp.where(sq == 0, 0.0, gch[0])
    gc[:, pl.ds(PAD + TOK, PAD)] = jnp.where(sq == SEQ - 1, 0.0, gch[1])

    def back_rows(i, carry):
        rows = pl.ds(pl.multiple_of(i * 16, 16), 16)
        g = gc[rows, :]
        t = taps[rows, :]
        total = go_t[rows, :].astype(F32)
        for tap in range(KW):
            total = total + t[:, tap : tap + 1] * shifted(g, REACH - tap)[:, PAD : PAD + TOK]
        gi_t[rows, :] = total.astype(BF)
        return carry

    lax.fori_loop(0, W // 16, back_rows, 0)

    factor = 1.0 / math.sqrt(TOK * SEQ)
    for j in range(1, SEQ):
        gk_in(j).wait_recv()
    total = gkr[0]
    for j in range(1, SEQ):
        total = total + gkr[j]
    gk[...] = total * factor

    ring_step(7)
    x_swap().wait_recv()
    gu[...] = (wf[z, xl, 0] + x_r[0].astype(F32)) * factor
    gd[...] = (wf[z, xl, 1] + x_r[1].astype(F32)) * factor

    for d in range(2):
        halo(d).wait_send()
        ghalo(d).wait_send()
    for i in range(3):
        weight(i).wait_send()
    for j in range(1, TP):
        stat_out(j).wait_send()
        bstat_out(j).wait_send()
    for j in range(1, SEQ):
        gk_out(j).wait_send()

    def drain(c, carry):
        for a in range(2):
            for j in range(3):
                ag1(a, c, j).wait_send()
            for d in range(2):
                ag2(a, c, d).wait_send()
                ag3(a, c, d).wait_send()
        for d in range(2):
            rs1(c, d).wait_send()
            rs2(c, d).wait_send()
        for j in range(3):
            rs3(c, j).wait_send()
        return carry

    lax.fori_loop(0, NC, drain, 0)
    for i in range(NZ):
        core_w(i).wait_send()
    for d in range(2):
        for step in range(4):
            for e in range(2):
                ring(d, step, e).wait_send()
    x_swap().wait_send()


def block(inputs, grad_out, kernel, ln_gain, layer_scale, w_up, w_down):
    start = lax.axis_index("tp") * W
    gain_l = lax.dynamic_slice_in_dim(ln_gain, start, W, 0)[:, None]
    scale_l = lax.dynamic_slice_in_dim(layer_scale, start, W, 0)[:, None]
    dma, vmem = pltpu.SemaphoreType.DMA, pltpu.VMEM
    scratch = [
        vmem((2, NC, W, TC), BF),
        vmem((2, NC, W, TC), BF),
        vmem((NC, D, TC), BF),
        vmem((NC, D, TC), BF),
        vmem((W, TOK + 2 * PAD), F32),
        vmem((W, TOK), F32),
        vmem((2, W, PAD), BF),
        vmem((2, TOK), F32),
        vmem((TP, 2, TOK), F32),
        vmem((2, TOK), F32),
        vmem((D, U), BF),
        vmem((U, D), BF),
        vmem((U, D), BF),
        vmem((U, TC), F32),
        vmem((U, TC), F32),
        vmem((NC, 2 * U, TC), BF),
        vmem((NC, 2 * U, TC), BF),
        vmem((NC, D, TC), F32),
        vmem((2, NC, 2 * W, TC), BF),
        vmem((2, NC, 2 * W, TC), BF),
        vmem((2, NC, 4 * W, TC), BF),
        vmem((2, NC, 4 * W, TC), BF),
        vmem((NC, 3, W, TC), BF),
        vmem((NC, 3, W, TC), BF),
        vmem((NC, W, TC), F32),
        vmem((2, HALF), F32),
        vmem((TP, 2, HALF), F32),
        vmem((W, TOK + 2 * PAD), F32),
        vmem((2, W, PAD), F32),
        vmem((2, W, PAD), F32),
        vmem((128, 128), F32),
        vmem((16, 128), F32),
        vmem((SEQ, 16, 128), F32),
        vmem((NZ, 2, 2, W, U), F32),
        vmem((NZ, 2, 2, W, U), BF),
        vmem((NZ, 2, 2, W, U), BF),
        vmem((2, 4, 2, 2, W, U), BF),
        vmem((2, 4, 2, 2, W, U), BF),
        vmem((2, W, U), BF),
        vmem((2, W, U), BF),
    ]
    for count in (2, 3, TP, 6 * NC, 4 * NC, 4 * NC, 2 * NC, 2 * NC, 3 * NC, TP, 2, SEQ, NZ, 16, 1):
        scratch += [dma((count,)), dma((count,))]
    spec = pl.BlockSpec(memory_space=pltpu.VMEM)
    gi_t, gu, gd, gk = pl.pallas_call(
        body,
        out_shape=[
            jax.ShapeDtypeStruct((W, TOK), BF),
            jax.ShapeDtypeStruct((W, U), F32),
            jax.ShapeDtypeStruct((W, U), F32),
            jax.ShapeDtypeStruct((16, 128), F32),
        ],
        in_specs=[spec] * 9,
        out_specs=[spec] * 4,
        scratch_shapes=scratch,
        compiler_params=pltpu.CompilerParams(
            collective_id=0, has_side_effects=True, vmem_limit_bytes=60 * 2**20
        ),
    )(
        inputs.T, grad_out.T, kernel.T, gain_l, scale_l, ln_gain[:, None], w_up, w_up.T, w_down,
    )
    return gi_t.T, gu, gd, gk[:KW, :W]


def solution(mesh):
    in_specs = (
        P("seq", "tp"),
        P("seq", "tp"),
        P(None, "tp"),
        P(),
        P(),
        P(None, "tp"),
        P("tp", None),
    )
    out_specs = (P("seq", "tp"), P("seq", "tp"), P("seq", "tp"), P(None, "tp"))
    return jax.shard_map(block, mesh=mesh, in_specs=in_specs, out_specs=out_specs, check_vma=False)
```

```python
import math

import jax
import jax.numpy as jnp
from jax import lax
from jax.experimental import pallas as pl
from jax.experimental.pallas import tpu as pltpu
from jax.sharding import PartitionSpec as P

MESH = pl.DeviceIdType.MESH
BF = jnp.bfloat16
F32 = jnp.float32

TP = 16
NY = 4
SEQ = 16
NZ = 8
W = 96
D = 1536
TOK = 2048
HALF = TOK // 2
NC = 4
TC = HALF // NC
U = 384
KW = 15
EDGE = 8
ROWS = 128

X_FIRST = ((False, True, True, True), (True, False, False, True))


def nn(a, b):
    return jnp.dot(a, b, preferred_element_type=F32)


def nt(a, b):
    return lax.dot_general(a, b, (((1,), (1,)), ((), ())), preferred_element_type=F32)


def body(
    x_in, go, taps, gain, scale, wu, wd,
    gi, gu, gd, gk,
    s_st, n_st, g_s, g_n, xp, cv, hin, st_s, st_1, st_m, st_2, mr, cols, gb, wu_t, wu_p, wu_tp,
    wd_p, pre_s, gh_s, hid, gpr, pf, s1, r1, s2, r2, s3, r3, own, bst, b_1, b_m, b_2, gc, gch,
    gks, gk_1, gk_m, gk_2, wf, c_s, c_r, z_s, z_r, x_s, x_r,
    halo_ss, halo_rs, w_ss, w_rs, st_ss, st_rs, ag_ss, ag_rs,
    r1_ss, r1_rs, r2_ss, r2_rs, r3_ss, r3_rs, b_ss, b_rs, gh_ss, gh_rs, gk_ss, gk_rs,
    c_ss, c_rs, z_ss, z_rs, x_ss, x_rs,
):
    tp = lax.axis_index("tp")
    sq = lax.axis_index("seq")
    k = lax.rem(tp, 2)
    xh = lax.rem(tp // 2, 2)
    y = tp // 4
    xl = sq // NZ
    z = lax.rem(sq, NZ)
    sent = []

    def at(y_, xh_, k_):
        return {"seq": sq, "tp": (y_ * 2 + xh_) * 2 + k_}

    def send(src, dst, ss, rs, dev):
        return pltpu.make_async_remote_copy(
            src_ref=src, dst_ref=dst, send_sem=ss, recv_sem=rs, device_id=dev, device_id_type=MESH
        )

    def go_out(copy):
        copy.start()
        sent.append(copy)

    up, down = lax.rem(y + 1, NY), lax.rem(y + NY - 1, NY)
    anti = lax.rem(y + 2, NY)
    y_dev = (at(up, xh, k), at(down, xh, k), at(anti, xh, k))
    other = 1 - k
    near = (at(y, 1 - xh, k), at(y, xh, other), at(y, 1 - xh, other))
    sq_next, sq_prev = lax.rem(sq + 1, SEQ), lax.rem(sq + SEQ - 1, SEQ)
    sq_dev = ({"seq": sq_next, "tp": tp}, {"seq": sq_prev, "tp": tp})
    z_dev = [{"seq": xl * NZ + lax.rem(z + j, NZ), "tp": tp} for j in range(NZ)]
    z_ring = (z_dev[1], z_dev[NZ - 1])
    x_dev = {"seq": (1 - xl) * NZ + z, "tp": tp}

    def rows_at(first, count):
        return pl.ds(pl.multiple_of(first, 32), count)

    def y_rows(which, first=0, count=4 * W):
        return rows_at(which * (4 * W) + first, count)

    def pair_rows(which, first=0, count=2 * W):
        return rows_at(which * (4 * W) + xh * (2 * W) + first, count)

    my_rows = rows_at(tp * W, W)

    barrier = pltpu.get_barrier_semaphore()
    partners = [*near, *y_dev, *sq_dev, *z_dev[1:], x_dev]
    for dev in partners:
        pl.semaphore_signal(barrier, inc=1, device_id=dev, device_id_type=MESH)

    def halo(d):
        src = x_in.at[pl.ds(TOK - 16, 16)] if d == 0 else x_in.at[pl.ds(0, 16)]
        return send(src, hin.at[d], halo_ss.at[d], halo_rs.at[d], sq_dev[d])

    def weight(i):
        src, dst = ((wd, wd_p), (wu, wu_p), (wu_t, wu_tp))[i]
        return send(src, dst, w_ss.at[i], w_rs.at[i], near[1])

    def stat(stage, j):
        src, dst, dev = ((st_s, st_1, near), (st_m, st_2, y_dev))[stage]
        i = stage * 3 + j
        return send(src, dst.at[j], st_ss.at[i], st_rs.at[i], dev[j])

    def bstat(stage, j):
        src, dst, dev = ((bst, b_1, y_dev), (b_m, b_2, near))[stage]
        i = stage * 3 + j
        return send(src, dst.at[j], b_ss.at[i], b_rs.at[i], dev[j])

    staged, full = (s_st, n_st), (g_s, g_n)

    def gather(a, c, slot):
        i = (a * NC + c) * 10 + slot
        buf = full[a].at[c]
        if slot < 3:
            src = staged[a].at[k if slot == 0 else other, c]
            return send(src, buf.at[my_rows], ag_ss.at[i], ag_rs.at[i], near[slot])
        if X_FIRST[a][c]:
            part, dev = (
                (y_rows(y), y_dev[0]),
                (y_rows(y), y_dev[1]),
                (y_rows(down, 0, 2 * W), y_dev[0]),
                (y_rows(up, 2 * W, 2 * W), y_dev[1]),
            )[slot - 3]
        else:
            part, dev = (
                (pair_rows(y), y_dev[0]),
                (pair_rows(y), y_dev[1]),
                (pair_rows(down, 0, W), y_dev[0]),
                (pair_rows(up, W, W), y_dev[1]),
                (pair_rows(y), near[0]),
                (pair_rows(down), near[0]),
                (pair_rows(up), near[0]),
            )[slot - 3]
        part = buf.at[part]
        return send(part, part, ag_ss.at[i], ag_rs.at[i], dev)

    def gather_last(a, c, d):
        i = (a * NC + c) * 2 + d
        part = full[a].at[c].at[pair_rows(anti, d * W, W)]
        i = 2 * NC * 10 + i
        return send(part, part, ag_ss.at[i], ag_rs.at[i], near[0])

    def gather_0(a, c):
        for slot in (2, 0, 1) if X_FIRST[a][c] else (1,):
            go_out(gather(a, c, slot))
        full[a][c, my_rows] = staged[a][k, c]

    def gather_1(a, c):
        for slot in (2, 0, 1) if X_FIRST[a][c] else (1,):
            gather(a, c, slot).wait_recv()
        go_out(gather(a, c, 3))
        go_out(gather(a, c, 4))
        if not X_FIRST[a][c]:
            go_out(gather(a, c, 7))

    def gather_2(a, c):
        for d in range(2):
            gather(a, c, 3 + d).wait_recv()
            go_out(gather(a, c, 5 + d))
            if not X_FIRST[a][c]:
                go_out(gather(a, c, 8 + d))

    def gather_3(a, c):
        if not X_FIRST[a][c]:
            for d in range(2):
                gather(a, c, 5 + d).wait_recv()
                go_out(gather_last(a, c, d))

    def gather_end(a, c):
        if X_FIRST[a][c]:
            for d in range(2):
                gather(a, c, 5 + d).wait_recv()
        else:
            for slot in (7, 8, 9):
                gather(a, c, slot).wait_recv()
            for d in range(2):
                gather_last(a, c, d).wait_recv()

    def rs1(c, d):
        i = c * 2 + d
        return send(s1.at[d, c], r1.at[d, c], r1_ss.at[i], r1_rs.at[i], y_dev[d])

    def rs2(c, d):
        i = c * 2 + d
        return send(s2.at[d, c], r2.at[d, c], r2_ss.at[i], r2_rs.at[i], y_dev[d])

    def rs3(c, j):
        i = c * 3 + j
        return send(s3.at[c, j], r3.at[c, j], r3_ss.at[i], r3_rs.at[i], near[j])

    def ghalo(d):
        src = gc.at[pl.ds(TOK, EDGE)] if d == 0 else gc.at[pl.ds(EDGE, EDGE)]
        return send(src, gch.at[d], gh_ss.at[d], gh_rs.at[d], sq_dev[d])

    def gk_x():
        return send(gks, gk_1, gk_ss.at[0], gk_rs.at[0], x_dev)

    def gk_z(j):
        return send(gk_m, gk_2.at[j], gk_ss.at[j], gk_rs.at[j], z_dev[j])

    def core_w(i):
        return send(c_s.at[i], c_r.at[i], c_ss.at[i], c_rs.at[i], near[1])

    def ring(d, step, e):
        i = (d * 4 + step) * 2 + e
        if step == 0:
            return send(
                z_s.at[d, step, e, pl.ds(d, 1)], z_r.at[d, step, e, pl.ds(d, 1)],
                z_ss.at[i], z_rs.at[i], z_ring[d],
            )
        return send(z_s.at[d, step, e], z_r.at[d, step, e], z_ss.at[i], z_rs.at[i], z_ring[d])

    def x_swap():
        return send(x_s, x_r, x_ss.at[0], x_rs.at[0], x_dev)

    turn = lax.rem(D - tp * W, D)
    scale_row = pltpu.roll(jnp.broadcast_to(scale[...], (8, D)), turn, 1)[0:1, 0:W]
    gain_row = pltpu.roll(jnp.broadcast_to(gain[...], (8, D)), turn, 1)[0:1, 0:128]
    cols[...] = jnp.broadcast_to(gain_row, (128, 128)).T
    for c in range(NC):
        for h in range(2):
            rows = pl.ds(h * HALF + c * TC, TC)
            s_st[h, c] = (scale_row * go[rows, :].astype(F32)).T.astype(BF)

    pl.semaphore_wait(barrier, len(partners))
    for d in range(2):
        go_out(halo(d))
    for c in range(NC):
        gather_0(0, c)
    for i in range(2):
        go_out(weight(i))

    def load(i, carry):
        xp[pl.ds(pl.multiple_of(EDGE + i * ROWS, 8), ROWS), :] = x_in[
            pl.ds(pl.multiple_of(i * ROWS, ROWS), ROWS), :
        ].astype(F32)
        return carry

    lax.fori_loop(0, TOK // ROWS, load, 0)
    for d in range(2):
        halo(d).wait_recv()
    xp[0:EDGE, :] = jnp.where(sq == 0, 0.0, hin[0].astype(F32)[8:16])
    xp[pl.ds(EDGE + TOK, EDGE), :] = jnp.where(sq == SEQ - 1, 0.0, hin[1].astype(F32)[0:8])

    def conv_rows(i, carry):
        total = None
        for tap in range(KW):
            term = taps[tap : tap + 1, :] * xp[pl.ds(i * ROWS + tap + 1, ROWS), :]
            total = term if total is None else total + term
        out = total.T
        at_ = pl.ds(pl.multiple_of(i * ROWS, ROWS), ROWS)
        cv[:, at_] = out
        st_s[0:1, at_] = jnp.sum(out, axis=0, keepdims=True)
        st_s[1:2, at_] = jnp.sum(out * out, axis=0, keepdims=True)
        return carry

    lax.fori_loop(0, TOK // ROWS, conv_rows, 0)
    for j in range(3):
        go_out(stat(0, j))
    gather_1(0, 0)
    for j in range(3):
        stat(0, j).wait_recv()
    st_m[...] = (st_s[...] + st_1[1]) + (st_1[0] + st_1[2])
    for j in range(3):
        go_out(stat(1, j))
    gather_1(0, 1)
    for j in range(3):
        stat(1, j).wait_recv()
    totals = (st_m[...] + st_2[2]) + (st_2[0] + st_2[1])
    mean = totals[0:1] / D
    var = totals[1:2] / D - mean * mean
    mr[0:1, :] = mean
    mr[1:2, :] = lax.rsqrt(var + 1e-06)
    gain_col = cols[0:W, 0:1]
    for c in range(NC):
        for h in range(2):
            at_ = pl.ds(h * HALF + c * TC, TC)
            nhat = (cv[:, at_] - mr[0:1, at_]) * mr[1:2, at_]
            n_st[h, c] = (nhat * gain_col).astype(BF)
        gather_0(1, c)

    for c in range(2, NC):
        gather_1(0, c)

    for i in range(D // 128):
        part = slice(i * 128, (i + 1) * 128)
        wu_t[:, part] = wu[part, :].T
        gb[part, :] = jnp.broadcast_to(gain[0:1, part], (128, 128)).T
    go_out(weight(2))

    gather_2(0, 0)
    gather_1(1, 0)
    gather_2(0, 1)
    gather_1(1, 1)
    gather_3(0, 0)
    gather_2(0, 2)
    gather_1(1, 2)
    gather_2(0, 3)
    gather_1(1, 3)
    for i in range(3):
        weight(i).wait_recv()

    def cotangent(c):
        gather_end(0, c)
        gh_s[c, 0:U] = nn(wd[...], g_s[c])
        gh_s[c, U:] = nn(wd_p[...], g_s[c])

    def rs2_step(c):
        for d, to in ((0, up), (1, down)):
            rs1(c, d).wait_recv()
            a, b = d * 2 * W, (1 - d) * 2 * W
            got = pf[c, y_rows(to, a, 2 * W)] + r1[d, c].astype(F32)
            s2[d, c, pl.ds(a, 2 * W)] = got.astype(BF)
            s2[d, c, pl.ds(b, 2 * W)] = pf[c, y_rows(to, b, 2 * W)].astype(BF)
            go_out(rs2(c, d))

    def rs3_step(c):
        for d in range(2):
            rs2(c, d).wait_recv()

        def group(g):
            rows = rows_at(g * W, W)
            mine = pf[c, y_rows(y, g * W, W)]
            return mine + r2[0, c, rows].astype(F32) + r2[1, c, rows].astype(F32)

        for j, (xh_, k_) in ((2, (1 - xh, other)), (0, (1 - xh, k)), (1, (xh, other))):
            s3[c, j] = group(xh_ * 2 + k_).astype(BF)
            go_out(rs3(c, j))
        own[c] = group(xh * 2 + k)

    def layers(c):
        at_ = pl.ds(c * TC, TC)
        acc = jnp.zeros((8, TC), F32)
        for u, w_t in enumerate((wu_t, wu_tp)):
            pre_s[...] = nn(w_t[...], g_n[c])

            def act(i, acc, u=u):
                v = pre_s[rows_at(i * 32, 32), :]
                to = rows_at(u * U + i * 32, 32)
                phi = 0.5 + 0.5 * lax.erf(v * 0.7071067811865476)
                slope = phi + v * jnp.exp(-0.5 * v * v) * 0.3989422804014327
                gp = (gh_s[c, to] * slope).astype(BF)
                hid[to, at_] = (v * phi).astype(BF)
                gpr[to, at_] = gp
                return acc + jnp.sum((gp.astype(F32) * v).reshape(4, 8, TC), axis=0)

            acc = lax.fori_loop(0, U // 32, act, acc)
        bst[1:2, at_] = jnp.sum(acc, axis=0, keepdims=True)

    def back(c):
        at_ = pl.ds(c * TC, TC)
        acc = [jnp.zeros((8, 128), F32)] * (TC // 128)
        for r in range(NY):
            rows = pl.ds(r * 4 * W, 4 * W)
            p = nn(wu[rows, :], gpr[0:U, at_]) + nn(wu_p[rows, :], gpr[U:, at_])
            pf[c, rows] = p
            for h in range(TC // 128):
                term = gb[rows, :] * p[:, h * 128 : (h + 1) * 128]
                acc[h] = acc[h] + jnp.sum(term.reshape(4 * W // 8, 8, 128), axis=0)
        for h in range(TC // 128):
            bst[0:1, pl.ds(c * TC + h * 128, 128)] = jnp.sum(acc[h], axis=0, keepdims=True)
        for d in range(2):
            s1[d, c] = pf[c, y_rows(anti, d * 2 * W, 2 * W)].astype(BF)
            go_out(rs1(c, d))

    cotangent(0)
    cotangent(1)
    gather_2(1, 0)
    cotangent(2)
    gather_2(1, 1)
    gather_3(1, 0)
    cotangent(3)
    gather_end(1, 0)
    layers(0)
    gather_3(1, 1)
    gather_2(1, 2)
    back(0)
    gather_2(1, 3)
    gather_end(1, 1)
    layers(1)
    gather_3(1, 2)
    back(1)
    rs2_step(0)
    gather_3(1, 3)
    gather_end(1, 2)
    layers(2)
    rs3_step(0)
    back(2)
    rs2_step(1)
    gather_end(1, 3)
    layers(3)
    back(3)
    for j in range(3):
        go_out(bstat(0, j))

    order = (4, 3, 5, 2, 6, 1, 7, 0)

    def weight_blocks(first, count):
        for a, (left, right) in enumerate(((g_n, gpr), (g_s, hid))):
            wide = []
            for c in range(NC):
                pieces = []
                for i in range(count):
                    b = lax.rem(z + order_at(first, i), NZ)
                    for e in range(2):
                        pieces.append(left[c, rows_at(e * (NZ * W) + b * W, W), :])
                wide.append(jnp.concatenate(pieces, axis=0))
            lhs = jnp.concatenate(wide, axis=1)
            theirs = nt(lhs, right[U:, :])
            mine = nt(lhs, right[0:U, :])
            for i in range(count):
                b = lax.rem(z + order_at(first, i), NZ)
                for e in range(2):
                    part = slice((i * 2 + e) * W, (i * 2 + e + 1) * W)
                    c_s[first + i, e, a] = theirs[part].astype(BF)
                    wf[b, e, a] = mine[part]
        for i in range(count):
            core_w(first + i).start()

    def order_at(first, i):
        return order[first + i]

    def ring_step(i):
        off = order[i]
        b = lax.rem(z + off, NZ)
        core_w(i).wait_recv()
        if off == 4:
            for e in range(2):
                for d in range(2):
                    got = wf[b, e, d] + c_r[i, e, d].astype(F32)
                    z_s[d, 0, e, d] = got.astype(BF)
                    go_out(ring(d, 0, e))
        elif off != 0:
            d = 0 if off < 4 else 1
            step = 4 - off if off < 4 else off - 4
            for e in range(2):
                ring(d, step - 1, e).wait_recv()
                for a in range(2):
                    got = wf[b, e, a] + c_r[i, e, a].astype(F32)
                    if step > 1 or a == d:
                        got = got + z_r[d, step - 1, e, a].astype(F32)
                    z_s[d, step, e, a] = got.astype(BF)
                go_out(ring(d, step, e))
        else:
            for e in range(2):
                for d in range(2):
                    ring(d, 3, e).wait_recv()

            def part(e, a):
                got = wf[b, e, a] + c_r[i, e, a].astype(F32)
                return got + z_r[0, 3, e, a].astype(F32) + z_r[1, 3, e, a].astype(F32)

            for a in range(2):
                x_s[a] = part(1 - xl, a).astype(BF)
            go_out(x_swap())
            for a in range(2):
                wf[b, xl, a] = part(xl, a)

    weight_blocks(0, 1)
    rs3_step(1)
    rs2_step(2)
    weight_blocks(1, 2)
    ring_step(0)
    rs2_step(3)
    rs3_step(2)
    ring_step(1)
    ring_step(2)
    weight_blocks(3, 2)
    for j in range(3):
        bstat(0, j).wait_recv()
    b_m[...] = (bst[...] + b_1[2]) + (b_1[0] + b_1[1])
    for j in range(3):
        go_out(bstat(1, j))
    rs3_step(3)
    weight_blocks(5, 3)
    ring_step(3)
    ring_step(4)

    for j in range(3):
        bstat(1, j).wait_recv()
    for c in range(NC):
        for j in range(3):
            rs3(c, j).wait_recv()
    sums_here = (b_m[...] + b_2[0]) / D
    sums_there = (b_2[1] + b_2[2]) / D
    for h in range(2):
        sums = jnp.where(k == h, sums_here, sums_there)
        for c in range(NC):
            at_ = pl.ds(h * HALF + c * TC, TC)
            rel = slice(c * TC, (c + 1) * TC)
            here = own[c] + r3[c, 0].astype(F32)
            there = r3[c, 1].astype(F32) + r3[c, 2].astype(F32)
            scaled_g = jnp.where(k == h, here, there) * gain_col
            rstd = mr[1:2, at_]
            nhat = (cv[:, at_] - mr[0:1, at_]) * rstd
            grad = rstd * (scaled_g - sums[0:1, rel] - nhat * sums[1:2, rel])
            gc[pl.ds(EDGE + h * HALF + c * TC, TC), :] = grad.T
    for d in range(2):
        go_out(ghalo(d))

    def tap_rows(i, sums):
        g = gc[pl.ds(pl.multiple_of(EDGE + i * ROWS, 8), ROWS), :]
        out = []
        for tap in range(KW):
            prod = g * xp[pl.ds(i * ROWS + tap + 1, ROWS), :]
            out.append(sums[tap] + jnp.sum(prod.reshape(ROWS // 8, 8, W), axis=0))
        return tuple(out)

    sums = lax.fori_loop(0, TOK // ROWS, tap_rows, (jnp.zeros((8, W), F32),) * KW)
    for tap in range(KW):
        gks[tap : tap + 1, :] = jnp.sum(sums[tap], axis=0, keepdims=True)
    gks[KW : KW + 1, :] = jnp.zeros((1, W), F32)
    go_out(gk_x())

    ring_step(5)
    ring_step(6)

    gk_x().wait_recv()
    gk_m[...] = gks[...] + gk_1[...]
    for j in range(1, NZ):
        go_out(gk_z(j))
    for d in range(2):
        ghalo(d).wait_recv()
    gc[0:EDGE, :] = jnp.where(sq == 0, 0.0, gch[0])
    gc[pl.ds(EDGE + TOK, EDGE), :] = jnp.where(sq == SEQ - 1, 0.0, gch[1])

    def back_rows(i, carry):
        at_ = pl.ds(pl.multiple_of(i * ROWS, ROWS), ROWS)
        total = go[at_, :].astype(F32)
        for tap in range(KW):
            total = total + taps[tap : tap + 1, :] * gc[pl.ds(i * ROWS + KW - tap, ROWS), :]
        gi[at_, :] = total.astype(BF)
        return carry

    lax.fori_loop(0, TOK // ROWS, back_rows, 0)

    factor = 1.0 / math.sqrt(TOK * SEQ)
    total = gk_m[...]
    for j in range(1, NZ):
        gk_z(j).wait_recv()
        total = total + gk_2[j]
    gk[...] = total[0:KW] * factor

    ring_step(7)
    x_swap().wait_recv()
    gu[...] = (wf[z, xl, 0] + x_r[0].astype(F32)) * factor
    gd[...] = (wf[z, xl, 1] + x_r[1].astype(F32)) * factor

    for copy in sent:
        copy.wait_send()
    for i in range(NZ):
        core_w(i).wait_send()


def block(inputs, grad_out, kernel, ln_gain, layer_scale, w_up, w_down):
    dma, vmem = pltpu.SemaphoreType.DMA, pltpu.VMEM
    scratch = [
        vmem((2, NC, W, TC), BF),
        vmem((2, NC, W, TC), BF),
        vmem((NC, D, TC), BF),
        vmem((NC, D, TC), BF),
        vmem((TOK + 2 * EDGE, W), F32),
        vmem((W, TOK), F32),
        vmem((2, 16, W), BF),
        vmem((2, TOK), F32),
        vmem((3, 2, TOK), F32),
        vmem((2, TOK), F32),
        vmem((3, 2, TOK), F32),
        vmem((2, TOK), F32),
        vmem((128, 128), F32),
        vmem((D, 128), F32),
        vmem((U, D), BF),
        vmem((D, U), BF),
        vmem((U, D), BF),
        vmem((U, D), BF),
        vmem((U, TC), F32),
        vmem((NC, 2 * U, TC), F32),
        vmem((2 * U, HALF), BF),
        vmem((2 * U, HALF), BF),
        vmem((NC, D, TC), F32),
        vmem((2, NC, 2 * W, TC), BF),
        vmem((2, NC, 2 * W, TC), BF),
        vmem((2, NC, 4 * W, TC), BF),
        vmem((2, NC, 4 * W, TC), BF),
        vmem((NC, 3, W, TC), BF),
        vmem((NC, 3, W, TC), BF),
        vmem((NC, W, TC), F32),
        vmem((2, HALF), F32),
        vmem((3, 2, HALF), F32),
        vmem((2, HALF), F32),
        vmem((3, 2, HALF), F32),
        vmem((TOK + 2 * EDGE, W), F32),
        vmem((2, EDGE, W), F32),
        vmem((16, W), F32),
        vmem((16, W), F32),
        vmem((16, W), F32),
        vmem((NZ, 16, W), F32),
        vmem((NZ, 2, 2, W, U), F32),
        vmem((NZ, 2, 2, W, U), BF),
        vmem((NZ, 2, 2, W, U), BF),
        vmem((2, 4, 2, 2, W, U), BF),
        vmem((2, 4, 2, 2, W, U), BF),
        vmem((2, W, U), BF),
        vmem((2, W, U), BF),
    ]
    for count in (2, 3, 6, 24 * NC, 2 * NC, 2 * NC, 3 * NC, 6, 2, NZ, NZ, 16, 1):
        scratch += [dma((count,)), dma((count,))]
    spec = pl.BlockSpec(memory_space=pltpu.VMEM)
    return pl.pallas_call(
        body,
        out_shape=[
            jax.ShapeDtypeStruct((TOK, W), BF),
            jax.ShapeDtypeStruct((W, U), F32),
            jax.ShapeDtypeStruct((W, U), F32),
            jax.ShapeDtypeStruct((KW, W), F32),
        ],
        in_specs=[spec] * 7,
        out_specs=[spec] * 4,
        scratch_shapes=scratch,
        compiler_params=pltpu.CompilerParams(
            collective_id=0, has_side_effects=True, vmem_limit_bytes=60 * 2**20
        ),
    )(inputs, grad_out, kernel, ln_gain[None, :], layer_scale[None, :], w_up, w_down)


def solution(mesh):
    in_specs = (
        P("seq", "tp"),
        P("seq", "tp"),
        P(None, "tp"),
        P(),
        P(),
        P(None, "tp"),
        P("tp", None),
    )
    out_specs = (P("seq", "tp"), P("seq", "tp"), P("seq", "tp"), P(None, "tp"))
    return jax.shard_map(block, mesh=mesh, in_specs=in_specs, out_specs=out_specs, check_vma=False)
```

```python
import math

import jax
import jax.numpy as jnp
from jax import lax
from jax.experimental import pallas as pl
from jax.experimental.pallas import tpu as pltpu
from jax.sharding import PartitionSpec as P

MESH = pl.DeviceIdType.MESH
BF = jnp.bfloat16
F32 = jnp.float32

TP = 16
NY = 4
SEQ = 16
NZ = 8
W = 96
D = 1536
TOK = 2048
HALF = TOK // 2
NC = 4
TC = HALF // NC
U = 384
KW = 15
EDGE = 8
ROWS = 128

X_FIRST = ((False, True, False, True), (True, False, True, True))


def nn(a, b):
    return jnp.dot(a, b, preferred_element_type=F32)


def nt(a, b):
    return lax.dot_general(a, b, (((1,), (1,)), ((), ())), preferred_element_type=F32)


def body(
    x_t, go_t, taps, gain, scale, wu_hbm, wd_hbm,
    gi_t, gu, gd, gk,
    s_st, n_st, g_s, g_n, xp, cv, h_st, hin, st_s, st_1, st_m, st_2, mr, cols, gb, wu, wd, wu_t, wu_p, wu_tp,
    wd_p, pre_s, hid, gpr, pf, s1, r1, s2, r2, s3, r3, own, bst, b_1, b_m, b_2, gc, gch,
    gks, gk_1, gk_m, gk_2, wf, c_s, c_r, z_s, z_r, x_s, x_r, e_s, e_r,
    halo_ss, halo_rs, w_ss, w_rs, st_ss, st_rs, ag_ss, ag_rs,
    r1_ss, r1_rs, r2_ss, r2_rs, r3_ss, r3_rs, b_ss, b_rs, gh_ss, gh_rs, gk_ss, gk_rs,
    c_ss, c_rs, z_ss, z_rs, x_ss, x_rs, e_ss, e_rs, in_ss, _,
):
    tp = lax.axis_index("tp")
    sq = lax.axis_index("seq")
    k = lax.rem(tp, 2)
    xh = lax.rem(tp // 2, 2)
    y = tp // 4
    xl = sq // NZ
    z = lax.rem(sq, NZ)
    sent = []

    def at(y_, xh_, k_):
        return {"seq": sq, "tp": (y_ * 2 + xh_) * 2 + k_}

    def send(src, dst, ss, rs, dev):
        return pltpu.make_async_remote_copy(
            src_ref=src, dst_ref=dst, send_sem=ss, recv_sem=rs, device_id=dev, device_id_type=MESH
        )

    def go_out(copy):
        copy.start()
        sent.append(copy)

    up, down = lax.rem(y + 1, NY), lax.rem(y + NY - 1, NY)
    anti = lax.rem(y + 2, NY)
    y_dev = (at(up, xh, k), at(down, xh, k), at(anti, xh, k))
    other = 1 - k
    near = (at(y, 1 - xh, k), at(y, xh, other), at(y, 1 - xh, other))
    sq_next, sq_prev = lax.rem(sq + 1, SEQ), lax.rem(sq + SEQ - 1, SEQ)
    sq_dev = ({"seq": sq_next, "tp": tp}, {"seq": sq_prev, "tp": tp})
    z_dev = [{"seq": xl * NZ + lax.rem(z + j, NZ), "tp": tp} for j in range(NZ)]
    z_ring = (z_dev[1], z_dev[NZ - 1])
    x_dev = {"seq": (1 - xl) * NZ + z, "tp": tp}

    def rows_at(first, count):
        return pl.ds(pl.multiple_of(first, 32), count)

    def y_rows(which, first=0, count=4 * W):
        return rows_at(which * (4 * W) + first, count)

    def pair_rows(which, first=0, count=2 * W):
        return rows_at(which * (4 * W) + xh * (2 * W) + first, count)

    my_rows = rows_at(tp * W, W)

    barrier = pltpu.get_barrier_semaphore()
    partners = [*near, *y_dev, *sq_dev, *z_dev[1:], x_dev]
    weights_in = (
        pltpu.make_async_copy(wu_hbm, wu, in_ss.at[0]),
        pltpu.make_async_copy(wd_hbm, wd, in_ss.at[1]),
    )
    for dev in partners:
        pl.semaphore_signal(barrier, inc=1, device_id=dev, device_id_type=MESH)

    for copy in weights_in:
        copy.start()

    def halo(d):
        return send(h_st.at[d], hin.at[d], halo_ss.at[d], halo_rs.at[d], sq_dev[d])

    def weight(i):
        src, dst = ((wd, wd_p), (wu, wu_p), (wu_t, wu_tp))[i]
        return send(src, dst, w_ss.at[i], w_rs.at[i], near[1])

    def stat(stage, j):
        src, dst, dev = ((st_s, st_1, near), (st_m, st_2, y_dev))[stage]
        i = stage * 3 + j
        return send(src, dst.at[j], st_ss.at[i], st_rs.at[i], dev[j])

    def bstat(stage, j):
        src, dst, dev = ((bst, b_1, y_dev), (b_m, b_2, near))[stage]
        i = stage * 3 + j
        return send(src, dst.at[j], b_ss.at[i], b_rs.at[i], dev[j])

    staged, full = (s_st, n_st), (g_s, g_n)

    def gather(a, c, slot):
        i = (a * NC + c) * 10 + slot
        buf = full[a].at[c]
        if slot < 3:
            src = staged[a].at[k if slot == 0 else other, c]
            return send(src, buf.at[my_rows], ag_ss.at[i], ag_rs.at[i], near[slot])
        if X_FIRST[a][c]:
            part, dev = (
                (y_rows(y), y_dev[0]),
                (y_rows(y), y_dev[1]),
                (y_rows(down, 0, 2 * W), y_dev[0]),
                (y_rows(up, 2 * W, 2 * W), y_dev[1]),
            )[slot - 3]
        else:
            part, dev = (
                (pair_rows(y), y_dev[0]),
                (pair_rows(y), y_dev[1]),
                (pair_rows(down, 0, W), y_dev[0]),
                (pair_rows(up, W, W), y_dev[1]),
                (pair_rows(y), near[0]),
                (pair_rows(down), near[0]),
                (pair_rows(up), near[0]),
            )[slot - 3]
        part = buf.at[part]
        return send(part, part, ag_ss.at[i], ag_rs.at[i], dev)

    def gather_last(a, c, d):
        i = (a * NC + c) * 2 + d
        part = full[a].at[c].at[pair_rows(anti, d * W, W)]
        i = 2 * NC * 10 + i
        return send(part, part, ag_ss.at[i], ag_rs.at[i], near[0])

    def gather_0(a, c):
        for slot in (2, 0, 1) if X_FIRST[a][c] else (1,):
            go_out(gather(a, c, slot))
        full[a][c, my_rows] = staged[a][k, c]

    def gather_1(a, c):
        for slot in (2, 0, 1) if X_FIRST[a][c] else (1,):
            gather(a, c, slot).wait_recv()
        go_out(gather(a, c, 3))
        go_out(gather(a, c, 4))
        if not X_FIRST[a][c]:
            go_out(gather(a, c, 7))

    def gather_2(a, c):
        for d in range(2):
            gather(a, c, 3 + d).wait_recv()
            go_out(gather(a, c, 5 + d))
            if not X_FIRST[a][c]:
                go_out(gather(a, c, 8 + d))

    def gather_3(a, c):
        if not X_FIRST[a][c]:
            for d in range(2):
                gather(a, c, 5 + d).wait_recv()
                go_out(gather_last(a, c, d))

    def gather_end(a, c):
        if X_FIRST[a][c]:
            for d in range(2):
                gather(a, c, 5 + d).wait_recv()
        else:
            for slot in (7, 8, 9):
                gather(a, c, slot).wait_recv()
            for d in range(2):
                gather_last(a, c, d).wait_recv()

    def rs1(c, d):
        i = c * 2 + d
        return send(s1.at[d, c], r1.at[d, c], r1_ss.at[i], r1_rs.at[i], y_dev[d])

    def rs2(c, d):
        i = c * 2 + d
        return send(s2.at[d, c], r2.at[d, c], r2_ss.at[i], r2_rs.at[i], y_dev[d])

    def rs3(c, j):
        i = c * 3 + j
        return send(s3.at[c, j], r3.at[c, j], r3_ss.at[i], r3_rs.at[i], near[j])

    def ghalo(d):
        src = gc.at[pl.ds(TOK, EDGE)] if d == 0 else gc.at[pl.ds(EDGE, EDGE)]
        return send(src, gch.at[d], gh_ss.at[d], gh_rs.at[d], sq_dev[d])

    def gk_x():
        return send(gks, gk_1, gk_ss.at[0], gk_rs.at[0], x_dev)

    def gk_z(j):
        return send(gk_m, gk_2.at[j], gk_ss.at[j], gk_rs.at[j], z_dev[j])

    def core_w(i, a):
        j = i * 2 + a
        return send(c_s.at[i, a], c_r.at[i, a], c_ss.at[j], c_rs.at[j], near[1])

    def ring(d, step, p):
        i = (d * 4 + step) * 3 + p
        src, dst = z_s.at[d, step, p], z_r.at[d, step, p]
        if step == 0 and p == 2:
            half = pl.ds(d * (W // 2), W // 2)
            src, dst = src.at[half], dst.at[half]
        return send(src, dst, z_ss.at[i], z_rs.at[i], z_ring[d])

    def x_early(i):
        return send(e_s.at[i], e_r.at[i], e_ss.at[i], e_rs.at[i], x_dev)

    def x_late():
        return send(x_s, x_r, x_ss.at[0], x_rs.at[0], x_dev)

    turn = lax.rem(D - tp * W, D)

    def local_column(ref):
        row = pltpu.roll(jnp.broadcast_to(ref[...].reshape(1, D), (8, D)), turn, 1)[0:1, 0:128]
        return jnp.broadcast_to(row, (128, 128)).T[0:W, 0:1]

    scale_col = local_column(scale)
    for c in range(NC):
        for h in range(2):
            at_ = pl.ds(h * HALF + c * TC, TC)
            s_st[h, c] = (scale_col * go_t[:, at_].astype(F32)).astype(BF)
    h_st[0] = x_t[:, pl.ds(TOK - 128, 128)].astype(F32).T[112:128].astype(BF)
    h_st[1] = x_t[:, pl.ds(0, 128)].astype(F32).T[0:16].astype(BF)
    cols[...] = jnp.broadcast_to(local_column(gain), (W, 128))

    def load(i, carry):
        block_t = x_t[:, pl.ds(pl.multiple_of(i * ROWS, ROWS), ROWS)].astype(F32)
        xp[pl.ds(pl.multiple_of(EDGE + i * ROWS, 8), ROWS), :] = block_t.T
        return carry

    steps = TOK // ROWS
    lax.fori_loop(0, steps, load, 0)
    pl.semaphore_wait(barrier, len(partners))
    for d in range(2):
        go_out(halo(d))
    for c in range(NC):
        gather_0(0, c)
    def conv_rows(i, carry):
        total = None
        for tap in range(KW):
            term = taps[tap : tap + 1, :] * xp[pl.ds(i * ROWS + tap + 1, ROWS), :]
            total = term if total is None else total + term
        out = total.T
        at_ = pl.ds(pl.multiple_of(i * ROWS, ROWS), ROWS)
        cv[:, at_] = out
        st_s[0:1, at_] = jnp.sum(out, axis=0, keepdims=True)
        st_s[1:2, at_] = jnp.sum(out * out, axis=0, keepdims=True)
        return carry

    lax.fori_loop(1, steps // 2, conv_rows, 0)
    gather_1(0, 0)
    for d in range(2):
        halo(d).wait_recv()
    xp[0:EDGE, :] = jnp.where(sq == 0, 0.0, hin[0].astype(F32)[8:16])
    xp[pl.ds(EDGE + TOK, EDGE), :] = jnp.where(sq == SEQ - 1, 0.0, hin[1].astype(F32)[0:8])
    gather_1(0, 1)
    conv_rows(0, 0)
    lax.fori_loop(steps // 2, steps, conv_rows, 0)
    for j in range(3):
        go_out(stat(0, j))
    gather_1(0, 2)
    gather_2(0, 0)
    gather_1(0, 3)
    for j in range(3):
        stat(0, j).wait_recv()
    st_m[...] = (st_s[...] + st_1[1]) + (st_1[0] + st_1[2])
    for j in range(3):
        go_out(stat(1, j))
    for copy in weights_in:
        copy.wait()
    for i in range(2):
        go_out(weight(i))
    gather_3(0, 0)

    for i in range(D // 128):
        part = slice(i * 128, (i + 1) * 128)
        wu_t[:, part] = wu[part, :].T
        gb[part, :] = jnp.broadcast_to(gain[part].reshape(1, 128), (128, 128)).T
    go_out(weight(2))

    for j in range(3):
        stat(1, j).wait_recv()
    totals = (st_m[...] + st_2[2]) + (st_2[0] + st_2[1])
    mean = totals[0:1] / D
    var = totals[1:2] / D - mean * mean
    mr[0:1, :] = mean
    mr[1:2, :] = lax.rsqrt(var + 1e-06)
    gain_col = cols[:, 0:1]
    for c in range(NC):
        for h in range(2):
            at_ = pl.ds(h * HALF + c * TC, TC)
            nhat = (cv[:, at_] - mr[0:1, at_]) * mr[1:2, at_]
            n_st[h, c] = (nhat * gain_col).astype(BF)
        gather_0(1, c)
    gather_2(0, 1)
    gather_1(1, 0)
    gather_2(0, 2)
    gather_3(0, 1)
    gather_1(1, 1)
    gather_2(0, 3)
    gather_3(0, 2)
    for i in range(3):
        weight(i).wait_recv()

    def cotangent(c):
        gather_end(0, c)
        pf[c, 0:U] = nn(wd[...], g_s[c])
        pf[c, U : 2 * U] = nn(wd_p[...], g_s[c])

    def rs2_step(c):
        for d, to in ((0, up), (1, down)):
            rs1(c, d).wait_recv()
            a, b = d * 2 * W, (1 - d) * 2 * W
            got = pf[c, y_rows(to, a, 2 * W)] + r1[d, c].astype(F32)
            s2[d, c, pl.ds(a, 2 * W)] = got.astype(BF)
            s2[d, c, pl.ds(b, 2 * W)] = pf[c, y_rows(to, b, 2 * W)].astype(BF)
            go_out(rs2(c, d))

    def rs3_step(c):
        for d in range(2):
            rs2(c, d).wait_recv()

        def group(g):
            rows = rows_at(g * W, W)
            mine = pf[c, y_rows(y, g * W, W)]
            return mine + r2[0, c, rows].astype(F32) + r2[1, c, rows].astype(F32)

        for j, (xh_, k_) in ((2, (1 - xh, other)), (0, (1 - xh, k)), (1, (xh, other))):
            s3[c, j] = group(xh_ * 2 + k_).astype(BF)
            go_out(rs3(c, j))
        own[c] = group(xh * 2 + k)

    def layers(c, u):
        at_ = pl.ds(c * TC, TC)
        pre_s[...] = nn((wu_t, wu_tp)[u][...], g_n[c])

        def act(i, acc):
            v = pre_s[rows_at(i * 32, 32), :]
            to = rows_at(u * U + i * 32, 32)
            phi = 0.5 + 0.5 * lax.erf(v * 0.7071067811865476)
            slope = phi + v * jnp.exp(-0.5 * v * v) * 0.3989422804014327
            gp = (pf[c, to] * slope).astype(BF)
            hid[to, at_] = (v * phi).astype(BF)
            gpr[to, at_] = gp
            return acc + jnp.sum((gp.astype(F32) * v).reshape(4, 8, TC), axis=0)

        acc = lax.fori_loop(0, U // 32, act, jnp.zeros((8, TC), F32))
        total = jnp.sum(acc, axis=0, keepdims=True)
        bst[1:2, at_] = total if u == 0 else bst[1:2, at_] + total

    def back(c):
        at_ = pl.ds(c * TC, TC)
        acc = [jnp.zeros((8, 128), F32)] * (TC // 128)
        for r in range(NY):
            rows = pl.ds(r * 4 * W, 4 * W)
            p = nn(wu[rows, :], gpr[0:U, at_]) + nn(wu_p[rows, :], gpr[U:, at_])
            pf[c, rows] = p
            for h in range(TC // 128):
                term = gb[rows, :] * p[:, h * 128 : (h + 1) * 128]
                acc[h] = acc[h] + jnp.sum(term.reshape(4 * W // 8, 8, 128), axis=0)
        for h in range(TC // 128):
            bst[0:1, pl.ds(c * TC + h * 128, 128)] = jnp.sum(acc[h], axis=0, keepdims=True)
        for d in range(2):
            s1[d, c] = pf[c, y_rows(anti, d * 2 * W, 2 * W)].astype(BF)
            go_out(rs1(c, d))

    cotangent(0)
    cotangent(1)
    gather_2(1, 0)
    gather_1(1, 2)
    gather_3(0, 3)
    cotangent(2)
    gather_2(1, 1)
    gather_3(1, 0)
    gather_1(1, 3)
    cotangent(3)
    gather_3(1, 1)
    gather_end(1, 0)
    layers(0, 0)
    gather_2(1, 2)
    layers(0, 1)
    gather_3(1, 2)
    back(0)
    gather_end(1, 1)
    layers(1, 0)
    gather_2(1, 3)
    layers(1, 1)
    gather_3(1, 3)
    back(1)
    rs2_step(0)
    gather_end(1, 2)
    layers(2, 0)
    layers(2, 1)
    back(2)
    rs2_step(1)
    gather_end(1, 3)
    layers(3, 0)
    rs3_step(0)
    layers(3, 1)

    order = (4, 3, 5, 2, 6, 1, 7, 0)

    def place(i):
        return lax.rem(z + order[i], NZ)

    def weight_blocks(first, count):
        for a, left, right in ((1, g_s, hid), (0, g_n, gpr)):
            wide = []
            for c in range(NC):
                pieces = []
                for i in range(first, first + count):
                    for e in range(2):
                        pieces.append(left[c, rows_at(e * (NZ * W) + place(i) * W, W), :])
                wide.append(jnp.concatenate(pieces, axis=0))
            lhs = jnp.concatenate(wide, axis=1)
            theirs = nt(lhs, right[U:, :])
            for j in range(2 * count):
                c_s[first + j // 2, a, j % 2] = theirs[j * W : (j + 1) * W].astype(BF)
            for i in range(first, first + count):
                go_out(core_w(i, a))
            mine = nt(lhs, right[0:U, :])
            for j in range(2 * count):
                wf[first + j // 2, a, j % 2] = mine[j * W : (j + 1) * W]

    def both_cores(i, a, e):
        return wf[i, a, e] + c_r[i, a, e].astype(F32)

    def over_x(i):
        core_w(i, 1).wait_recv()
        e_s[i] = both_cores(i, 1, 1 - xl).astype(BF)
        go_out(x_early(i))

    def way(i):
        off = order[i]
        return (0, 4 - off) if off < 4 else (1, off - 4)

    def ring_up(i):
        core_w(i, 0).wait_recv()
        if order[i] == 4:
            for d in range(2):
                z_s[d, 0, d] = both_cores(i, 0, d).astype(BF)
                go_out(ring(d, 0, d))
        elif order[i] != 0:
            d, step = way(i)
            for e in (d, 1 - d):
                got = both_cores(i, 0, e)
                if step > 1 or e == d:
                    ring(d, step - 1, e).wait_recv()
                    got = got + z_r[d, step - 1, e].astype(F32)
                z_s[d, step, e] = got.astype(BF)
                go_out(ring(d, step, e))
        else:
            for e in range(2):
                for d in range(2):
                    ring(d, 3, e).wait_recv()

            def part(e):
                return both_cores(i, 0, e) + z_r[0, 3, e].astype(F32) + z_r[1, 3, e].astype(F32)

            x_s[...] = part(1 - xl).astype(BF)
            go_out(x_late())
            gu[...] = part(xl)

    def ring_down(i):
        x_early(i).wait_recv()
        mine = both_cores(i, 1, xl) + e_r[i].astype(F32)
        halves = (slice(0, W // 2), slice(W // 2, W))
        if order[i] == 4:
            for d, half in enumerate(halves):
                z_s[d, 0, 2, half] = mine[half].astype(BF)
                go_out(ring(d, 0, 2))
        elif order[i] != 0:
            d, step = way(i)
            ring(d, step - 1, 2).wait_recv()
            if step == 1:
                half, rest = halves[d], halves[1 - d]
                z_s[d, 1, 2, half] = (mine[half] + z_r[d, 0, 2, half].astype(F32)).astype(BF)
                z_s[d, 1, 2, rest] = mine[rest].astype(BF)
            else:
                z_s[d, step, 2] = (mine + z_r[d, step - 1, 2].astype(F32)).astype(BF)
            go_out(ring(d, step, 2))
        else:
            for d in range(2):
                ring(d, 3, 2).wait_recv()
            gd[...] = factor * (mine + z_r[0, 3, 2].astype(F32) + z_r[1, 3, 2].astype(F32))

    factor = 1.0 / math.sqrt(TOK * SEQ)
    weight_blocks(0, 1)
    back(3)
    for j in range(3):
        go_out(bstat(0, j))
    over_x(0)
    ring_up(0)
    rs2_step(2)
    weight_blocks(1, 2)
    ring_down(0)
    over_x(1)
    over_x(2)
    rs2_step(3)
    ring_up(1)
    ring_up(2)
    rs3_step(1)
    for j in range(3):
        bstat(0, j).wait_recv()
    b_m[...] = (bst[...] + b_1[2]) + (b_1[0] + b_1[1])
    for j in range(3):
        go_out(bstat(1, j))
    weight_blocks(3, 2)
    ring_down(1)
    ring_down(2)
    over_x(3)
    over_x(4)
    rs3_step(2)
    ring_up(3)
    ring_up(4)
    rs3_step(3)
    weight_blocks(5, 2)
    ring_down(3)
    ring_down(4)
    over_x(5)
    over_x(6)

    for j in range(3):
        bstat(1, j).wait_recv()
    for c in range(NC):
        for j in range(3):
            rs3(c, j).wait_recv()
    sums_here = (b_m[...] + b_2[0]) / D
    sums_there = (b_2[1] + b_2[2]) / D
    for h in range(2):
        sums = jnp.where(k == h, sums_here, sums_there)
        for c in range(NC):
            at_ = pl.ds(h * HALF + c * TC, TC)
            rel = slice(c * TC, (c + 1) * TC)
            here = own[c] + r3[c, 0].astype(F32)
            there = r3[c, 1].astype(F32) + r3[c, 2].astype(F32)
            scaled_g = jnp.where(k == h, here, there) * gain_col
            rstd = mr[1:2, at_]
            nhat = (cv[:, at_] - mr[0:1, at_]) * rstd
            grad = rstd * (scaled_g - sums[0:1, rel] - nhat * sums[1:2, rel])
            gc[pl.ds(EDGE + h * HALF + c * TC, TC), :] = grad.T
    for d in range(2):
        go_out(ghalo(d))
    ring_up(5)
    ring_up(6)
    weight_blocks(7, 1)
    ring_down(5)
    ring_down(6)
    over_x(7)

    def tap_rows(i, sums):
        g = gc[pl.ds(pl.multiple_of(EDGE + i * ROWS, 8), ROWS), :]
        out = []
        for tap in range(KW):
            prod = g * xp[pl.ds(i * ROWS + tap + 1, ROWS), :]
            out.append(sums[tap] + jnp.sum(prod.reshape(ROWS // 8, 8, W), axis=0))
        return tuple(out)

    sums = lax.fori_loop(0, TOK // ROWS, tap_rows, (jnp.zeros((8, W), F32),) * KW)
    for tap in range(KW):
        gks[tap : tap + 1, :] = jnp.sum(sums[tap], axis=0, keepdims=True)
    gks[KW : KW + 1, :] = jnp.zeros((1, W), F32)
    go_out(gk_x())


    ring_up(7)

    gk_x().wait_recv()
    gk_m[...] = gks[...] + gk_1[...]
    for j in range(1, NZ):
        go_out(gk_z(j))
    for d in range(2):
        ghalo(d).wait_recv()
    gc[0:EDGE, :] = jnp.where(sq == 0, 0.0, gch[0])
    gc[pl.ds(EDGE + TOK, EDGE), :] = jnp.where(sq == SEQ - 1, 0.0, gch[1])

    def back_rows(i, carry):
        at_ = pl.ds(pl.multiple_of(i * ROWS, ROWS), ROWS)
        total = None
        for tap in range(KW):
            term = taps[tap : tap + 1, :] * gc[pl.ds(i * ROWS + KW - tap, ROWS), :]
            total = term if total is None else total + term
        gi_t[:, at_] = (go_t[:, at_].astype(F32) + total.T).astype(BF)
        return carry

    lax.fori_loop(0, TOK // ROWS, back_rows, 0)

    total = gk_m[...]
    for j in range(1, NZ):
        gk_z(j).wait_recv()
        total = total + gk_2[j]
    gk[...] = total[0:KW] * factor

    ring_down(7)
    x_late().wait_recv()
    gu[...] = (gu[...] + x_r[...].astype(F32)) * factor

    for copy in sent:
        copy.wait_send()


def hand_on(*arrays):
    def copy_all(*refs):
        n = len(arrays)
        for src, dst in zip(refs[:n], refs[n:]):
            dst[...] = src[...]

    spec = pl.BlockSpec(memory_space=pltpu.VMEM)
    return pl.pallas_call(
        copy_all,
        out_shape=[jax.ShapeDtypeStruct(a.shape, a.dtype) for a in arrays],
        in_specs=[spec] * len(arrays),
        out_specs=[spec] * len(arrays),
    )(*arrays)


def block(inputs, grad_out, kernel, ln_gain, layer_scale, w_up, w_down):
    dma, vmem = pltpu.SemaphoreType.DMA, pltpu.VMEM
    scratch = [
        vmem((2, NC, W, TC), BF),
        vmem((2, NC, W, TC), BF),
        vmem((NC, D, TC), BF),
        vmem((NC, D, TC), BF),
        vmem((TOK + 2 * EDGE, W), F32),
        vmem((W, TOK), F32),
        vmem((2, 16, W), BF),
        vmem((2, 16, W), BF),
        vmem((2, TOK), F32),
        vmem((3, 2, TOK), F32),
        vmem((2, TOK), F32),
        vmem((3, 2, TOK), F32),
        vmem((2, TOK), F32),
        vmem((W, 128), F32),
        vmem((D, 128), F32),
        vmem((D, U), BF),
        vmem((U, D), BF),
        vmem((U, D), BF),
        vmem((D, U), BF),
        vmem((U, D), BF),
        vmem((U, D), BF),
        vmem((U, TC), F32),
        vmem((2 * U, HALF), BF),
        vmem((2 * U, HALF), BF),
        vmem((NC, D, TC), F32),
        vmem((2, NC, 2 * W, TC), BF),
        vmem((2, NC, 2 * W, TC), BF),
        vmem((2, NC, 4 * W, TC), BF),
        vmem((2, NC, 4 * W, TC), BF),
        vmem((NC, 3, W, TC), BF),
        vmem((NC, 3, W, TC), BF),
        vmem((NC, W, TC), F32),
        vmem((2, HALF), F32),
        vmem((3, 2, HALF), F32),
        vmem((2, HALF), F32),
        vmem((3, 2, HALF), F32),
        vmem((TOK + 2 * EDGE, W), F32),
        vmem((2, EDGE, W), F32),
        vmem((16, W), F32),
        vmem((16, W), F32),
        vmem((16, W), F32),
        vmem((NZ, 16, W), F32),
        vmem((NZ, 2, 2, W, U), F32),
        vmem((NZ, 2, 2, W, U), BF),
        vmem((NZ, 2, 2, W, U), BF),
        vmem((2, 4, 3, W, U), BF),
        vmem((2, 4, 3, W, U), BF),
        vmem((W, U), BF),
        vmem((W, U), BF),
        vmem((NZ, W, U), BF),
        vmem((NZ, W, U), BF),
    ]
    for count in (2, 3, 6, 24 * NC, 2 * NC, 2 * NC, 3 * NC, 6, 2, NZ, 2 * NZ, 24, 1, NZ, 2):
        scratch += [dma((count,)), dma((count,))]
    spec = pl.BlockSpec(memory_space=pltpu.VMEM)
    gi_t, gu, gd, gk = pl.pallas_call(
        body,
        out_shape=[
            jax.ShapeDtypeStruct((W, TOK), BF),
            jax.ShapeDtypeStruct((W, U), F32),
            jax.ShapeDtypeStruct((W, U), F32),
            jax.ShapeDtypeStruct((KW, W), F32),
        ],
        in_specs=[spec] * 5 + [pl.BlockSpec(memory_space=pl.ANY)] * 2,
        out_specs=[spec] * 4,
        scratch_shapes=scratch,
        compiler_params=pltpu.CompilerParams(
            collective_id=0, has_side_effects=True, vmem_limit_bytes=60 * 2**20
        ),
    )(inputs.T, grad_out.T, kernel, ln_gain, layer_scale, w_up, w_down)
    gi_t, gu, gd, gk = hand_on(gi_t, gu, gd, gk)
    return gi_t.T, gu, gd, gk


def solution(mesh):
    in_specs = (
        P("seq", "tp"),
        P("seq", "tp"),
        P(None, "tp"),
        P(),
        P(),
        P(None, "tp"),
        P("tp", None),
    )
    out_specs = (P("seq", "tp"), P("seq", "tp"), P("seq", "tp"), P(None, "tp"))
    return jax.shard_map(block, mesh=mesh, in_specs=in_specs, out_specs=out_specs, check_vma=False)
```

```python
import math

import jax
import jax.numpy as jnp
from jax import lax
from jax.experimental import pallas as pl
from jax.experimental.pallas import tpu as pltpu
from jax.sharding import PartitionSpec as P

MESH = pl.DeviceIdType.MESH
BF = jnp.bfloat16
F32 = jnp.float32

TP = 16
NY = 4
SEQ = 16
NZ = 8
W = 96
D = 1536
TOK = 2048
HALF = TOK // 2
NC = 4
TC = HALF // NC
U = 384
KW = 15
EDGE = 8
ROWS = 128

X_FIRST = ((False, True, False, True), (False, True, True, True))


def nn(a, b):
    return jnp.dot(a, b, preferred_element_type=F32)


def nt(a, b):
    return lax.dot_general(a, b, (((1,), (1,)), ((), ())), preferred_element_type=F32)


def body(
    x_t, go_t, taps, gain, scale, wu_hbm, wd_hbm,
    gi_t, gu, gd, gk,
    s_st, n_st, g_s, g_n, xp, cv, h_st, hin, st_s, st_1, st_m, st_2, mr, cols, gb, wu, wd, wu_t, wu_p, wu_tp,
    wd_p, pre_s, hid, gpr, pf, s1, r1, s2, r2, s3, r3, own, bst, b_1, b_m, b_2, gc, gch,
    gks, gk_1, gk_m, gk_2, wf, c_s, c_r, z_s, z_r, x_s, x_r, e_s, e_r,
    halo_ss, halo_rs, w_ss, w_rs, st_ss, st_rs, ag_ss, ag_rs,
    r1_ss, r1_rs, r2_ss, r2_rs, r3_ss, r3_rs, b_ss, b_rs, gh_ss, gh_rs, gk_ss, gk_rs,
    c_ss, c_rs, z_ss, z_rs, x_ss, x_rs, e_ss, e_rs, in_ss, _,
):
    tp = lax.axis_index("tp")
    sq = lax.axis_index("seq")
    k = lax.rem(tp, 2)
    xh = lax.rem(tp // 2, 2)
    y = tp // 4
    xl = sq // NZ
    z = lax.rem(sq, NZ)
    sent = []

    def at(y_, xh_, k_):
        return {"seq": sq, "tp": (y_ * 2 + xh_) * 2 + k_}

    def send(src, dst, ss, rs, dev):
        return pltpu.make_async_remote_copy(
            src_ref=src, dst_ref=dst, send_sem=ss, recv_sem=rs, device_id=dev, device_id_type=MESH
        )

    def go_out(copy):
        copy.start()
        sent.append(copy)

    up, down = lax.rem(y + 1, NY), lax.rem(y + NY - 1, NY)
    anti = lax.rem(y + 2, NY)
    y_dev = (at(up, xh, k), at(down, xh, k), at(anti, xh, k))
    other = 1 - k
    near = (at(y, 1 - xh, k), at(y, xh, other), at(y, 1 - xh, other))
    sq_next, sq_prev = lax.rem(sq + 1, SEQ), lax.rem(sq + SEQ - 1, SEQ)
    sq_dev = ({"seq": sq_next, "tp": tp}, {"seq": sq_prev, "tp": tp})
    z_dev = [{"seq": xl * NZ + lax.rem(z + j, NZ), "tp": tp} for j in range(NZ)]
    z_ring = (z_dev[1], z_dev[NZ - 1])
    x_dev = {"seq": (1 - xl) * NZ + z, "tp": tp}

    def rows_at(first, count):
        return pl.ds(pl.multiple_of(first, 32), count)

    def y_rows(which, first=0, count=4 * W):
        return rows_at(which * (4 * W) + first, count)

    def pair_rows(which, first=0, count=2 * W):
        return rows_at(which * (4 * W) + xh * (2 * W) + first, count)

    my_rows = rows_at(tp * W, W)

    barrier = pltpu.get_barrier_semaphore()
    partners = [*near, *y_dev, *sq_dev, *z_dev[1:], x_dev]
    weights_in = (
        pltpu.make_async_copy(wu_hbm, wu, in_ss.at[0]),
        pltpu.make_async_copy(wd_hbm, wd, in_ss.at[1]),
    )
    for dev in partners:
        pl.semaphore_signal(barrier, inc=1, device_id=dev, device_id_type=MESH)

    for copy in weights_in:
        copy.start()

    def halo(d):
        return send(h_st.at[d], hin.at[d], halo_ss.at[d], halo_rs.at[d], sq_dev[d])

    def weight(i):
        src, dst = ((wd, wd_p), (wu, wu_p), (wu_t, wu_tp))[i]
        return send(src, dst, w_ss.at[i], w_rs.at[i], near[1])

    def stat(stage, j):
        src, dst, dev = ((st_s, st_1, near), (st_m, st_2, y_dev))[stage]
        i = stage * 3 + j
        return send(src, dst.at[j], st_ss.at[i], st_rs.at[i], dev[j])

    def bstat(stage, j):
        src, dst, dev = ((bst, b_1, y_dev), (b_m, b_2, near))[stage]
        i = stage * 3 + j
        return send(src, dst.at[j], b_ss.at[i], b_rs.at[i], dev[j])

    staged, full = (s_st, n_st), (g_s, g_n)

    def gather(a, c, slot):
        i = (a * NC + c) * 10 + slot
        buf = full[a].at[c]
        if slot < 3:
            src = staged[a].at[k if slot == 0 else other, c]
            return send(src, buf.at[my_rows], ag_ss.at[i], ag_rs.at[i], near[slot])
        if X_FIRST[a][c]:
            part, dev = (
                (y_rows(y), y_dev[0]),
                (y_rows(y), y_dev[1]),
                (y_rows(down, 0, 2 * W), y_dev[0]),
                (y_rows(up, 2 * W, 2 * W), y_dev[1]),
            )[slot - 3]
        else:
            part, dev = (
                (pair_rows(y), y_dev[0]),
                (pair_rows(y), y_dev[1]),
                (pair_rows(down, 0, W), y_dev[0]),
                (pair_rows(up, W, W), y_dev[1]),
                (pair_rows(y), near[0]),
                (pair_rows(down), near[0]),
                (pair_rows(up), near[0]),
            )[slot - 3]
        part = buf.at[part]
        return send(part, part, ag_ss.at[i], ag_rs.at[i], dev)

    def gather_last(a, c, d):
        i = (a * NC + c) * 2 + d
        part = full[a].at[c].at[pair_rows(anti, d * W, W)]
        i = 2 * NC * 10 + i
        return send(part, part, ag_ss.at[i], ag_rs.at[i], near[0])

    def gather_0(a, c):
        for slot in (2, 0, 1) if X_FIRST[a][c] else (1,):
            go_out(gather(a, c, slot))
        full[a][c, my_rows] = staged[a][k, c]

    def gather_1(a, c):
        for slot in (2, 0, 1) if X_FIRST[a][c] else (1,):
            gather(a, c, slot).wait_recv()
        go_out(gather(a, c, 3))
        go_out(gather(a, c, 4))
        if not X_FIRST[a][c]:
            go_out(gather(a, c, 7))

    def gather_2(a, c):
        for d in range(2):
            gather(a, c, 3 + d).wait_recv()
            go_out(gather(a, c, 5 + d))
            if not X_FIRST[a][c]:
                go_out(gather(a, c, 8 + d))

    def gather_3(a, c):
        if not X_FIRST[a][c]:
            for d in range(2):
                gather(a, c, 5 + d).wait_recv()
                go_out(gather_last(a, c, d))

    def gather_end(a, c):
        if X_FIRST[a][c]:
            for d in range(2):
                gather(a, c, 5 + d).wait_recv()
        else:
            for slot in (7, 8, 9):
                gather(a, c, slot).wait_recv()
            for d in range(2):
                gather_last(a, c, d).wait_recv()

    def rs1(c, d):
        i = c * 2 + d
        return send(s1.at[d, c], r1.at[d, c], r1_ss.at[i], r1_rs.at[i], y_dev[d])

    def rs2(c, d):
        i = c * 2 + d
        return send(s2.at[d, c], r2.at[d, c], r2_ss.at[i], r2_rs.at[i], y_dev[d])

    def rs3(c, j):
        i = c * 3 + j
        return send(s3.at[c, j], r3.at[c, j], r3_ss.at[i], r3_rs.at[i], near[j])

    def ghalo(d):
        src = gc.at[pl.ds(TOK, EDGE)] if d == 0 else gc.at[pl.ds(EDGE, EDGE)]
        return send(src, gch.at[d], gh_ss.at[d], gh_rs.at[d], sq_dev[d])

    def gk_x():
        return send(gks, gk_1, gk_ss.at[0], gk_rs.at[0], x_dev)

    def gk_z(j):
        return send(gk_m, gk_2.at[j], gk_ss.at[j], gk_rs.at[j], z_dev[j])

    def core_w(i, a):
        j = i * 2 + a
        return send(c_s.at[i, a], c_r.at[i, a], c_ss.at[j], c_rs.at[j], near[1])

    def ring(d, step, p):
        i = (d * 4 + step) * 3 + p
        src, dst = z_s.at[d, step, p], z_r.at[d, step, p]
        if step == 0 and p == 2:
            half = pl.ds(d * (W // 2), W // 2)
            src, dst = src.at[half], dst.at[half]
        return send(src, dst, z_ss.at[i], z_rs.at[i], z_ring[d])

    def x_early(i):
        return send(e_s.at[i], e_r.at[i], e_ss.at[i], e_rs.at[i], x_dev)

    def x_late():
        return send(x_s, x_r, x_ss.at[0], x_rs.at[0], x_dev)

    turn = lax.rem(D - tp * W, D)

    def local_column(ref):
        row = pltpu.roll(jnp.broadcast_to(ref[...].reshape(1, D), (8, D)), turn, 1)[0:1, 0:128]
        return jnp.broadcast_to(row, (128, 128)).T[0:W, 0:1]

    scale_col = local_column(scale)
    for c in range(NC):
        for h in range(2):
            at_ = pl.ds(h * HALF + c * TC, TC)
            s_st[h, c] = (scale_col * go_t[:, at_].astype(F32)).astype(BF)
    h_st[0] = x_t[:, pl.ds(TOK - 128, 128)].astype(F32).T[112:128].astype(BF)
    h_st[1] = x_t[:, pl.ds(0, 128)].astype(F32).T[0:16].astype(BF)
    cols[...] = jnp.broadcast_to(local_column(gain), (W, 128))

    def load(i, carry):
        block_t = x_t[:, pl.ds(pl.multiple_of(i * ROWS, ROWS), ROWS)].astype(F32)
        xp[pl.ds(pl.multiple_of(EDGE + i * ROWS, 8), ROWS), :] = block_t.T
        return carry

    steps = TOK // ROWS
    lax.fori_loop(0, steps, load, 0)
    pl.semaphore_wait(barrier, len(partners))
    for d in range(2):
        go_out(halo(d))
    for c in range(NC):
        gather_0(0, c)
    def conv_rows(i, carry):
        total = None
        for tap in range(KW):
            term = taps[tap : tap + 1, :] * xp[pl.ds(i * ROWS + tap + 1, ROWS), :]
            total = term if total is None else total + term
        out = total.T
        at_ = pl.ds(pl.multiple_of(i * ROWS, ROWS), ROWS)
        cv[:, at_] = out
        st_s[0:1, at_] = jnp.sum(out, axis=0, keepdims=True)
        st_s[1:2, at_] = jnp.sum(out * out, axis=0, keepdims=True)
        return carry

    lax.fori_loop(1, steps // 2, conv_rows, 0)
    gather_1(0, 0)
    for d in range(2):
        halo(d).wait_recv()
    xp[0:EDGE, :] = jnp.where(sq == 0, 0.0, hin[0].astype(F32)[8:16])
    xp[pl.ds(EDGE + TOK, EDGE), :] = jnp.where(sq == SEQ - 1, 0.0, hin[1].astype(F32)[0:8])
    gather_1(0, 1)
    conv_rows(0, 0)
    lax.fori_loop(steps // 2, steps, conv_rows, 0)
    for j in range(3):
        go_out(stat(0, j))
    gather_1(0, 2)
    gather_2(0, 0)
    gather_1(0, 3)
    for j in range(3):
        stat(0, j).wait_recv()
    st_m[...] = (st_s[...] + st_1[1]) + (st_1[0] + st_1[2])
    for j in range(3):
        go_out(stat(1, j))
    for copy in weights_in:
        copy.wait()
    for i in range(2):
        go_out(weight(i))
    gather_3(0, 0)

    for i in range(D // 128):
        part = slice(i * 128, (i + 1) * 128)
        wu_t[:, part] = wu[part, :].T
        gb[part, :] = jnp.broadcast_to(gain[part].reshape(1, 128), (128, 128)).T
    go_out(weight(2))

    for j in range(3):
        stat(1, j).wait_recv()
    totals = (st_m[...] + st_2[2]) + (st_2[0] + st_2[1])
    mean = totals[0:1] / D
    var = totals[1:2] / D - mean * mean
    mr[0:1, :] = mean
    mr[1:2, :] = lax.rsqrt(var + 1e-06)
    gain_col = cols[:, 0:1]
    for c in range(NC):
        for h in range(2):
            at_ = pl.ds(h * HALF + c * TC, TC)
            nhat = (cv[:, at_] - mr[0:1, at_]) * mr[1:2, at_]
            n_st[h, c] = (nhat * gain_col).astype(BF)
        gather_0(1, c)
    gather_2(0, 1)
    gather_1(1, 0)
    gather_2(0, 2)
    gather_3(0, 1)
    gather_1(1, 1)
    gather_2(0, 3)
    gather_3(0, 2)
    for i in range(3):
        weight(i).wait_recv()

    def cotangent(c):
        gather_end(0, c)
        pf[c, 0:U] = nn(wd[...], g_s[c])
        pf[c, U : 2 * U] = nn(wd_p[...], g_s[c])

    def rs2_step(c):
        for d, to in ((0, up), (1, down)):
            rs1(c, d).wait_recv()
            a, b = d * 2 * W, (1 - d) * 2 * W
            got = pf[c, y_rows(to, a, 2 * W)] + r1[d, c].astype(F32)
            s2[d, c, pl.ds(a, 2 * W)] = got.astype(BF)
            s2[d, c, pl.ds(b, 2 * W)] = pf[c, y_rows(to, b, 2 * W)].astype(BF)
            go_out(rs2(c, d))

    def rs3_step(c):
        for d in range(2):
            rs2(c, d).wait_recv()

        def group(g):
            rows = rows_at(g * W, W)
            mine = pf[c, y_rows(y, g * W, W)]
            return mine + r2[0, c, rows].astype(F32) + r2[1, c, rows].astype(F32)

        for j, (xh_, k_) in ((2, (1 - xh, other)), (0, (1 - xh, k)), (1, (xh, other))):
            s3[c, j] = group(xh_ * 2 + k_).astype(BF)
            go_out(rs3(c, j))
        own[c] = group(xh * 2 + k)

    def layers(c, u):
        at_ = pl.ds(c * TC, TC)
        pre_s[...] = nn((wu_t, wu_tp)[u][...], g_n[c])

        def act(i, acc):
            v = pre_s[rows_at(i * 32, 32), :]
            to = rows_at(u * U + i * 32, 32)
            phi = 0.5 + 0.5 * lax.erf(v * 0.7071067811865476)
            slope = phi + v * jnp.exp(-0.5 * v * v) * 0.3989422804014327
            gp = (pf[c, to] * slope).astype(BF)
            hid[to, at_] = (v * phi).astype(BF)
            gpr[to, at_] = gp
            return acc + jnp.sum((gp.astype(F32) * v).reshape(4, 8, TC), axis=0)

        acc = lax.fori_loop(0, U // 32, act, jnp.zeros((8, TC), F32))
        total = jnp.sum(acc, axis=0, keepdims=True)
        bst[1:2, at_] = total if u == 0 else bst[1:2, at_] + total

    def back(c):
        at_ = pl.ds(c * TC, TC)
        acc = [jnp.zeros((8, 128), F32)] * (TC // 128)
        for r in range(NY):
            rows = pl.ds(r * 4 * W, 4 * W)
            p = nn(wu[rows, :], gpr[0:U, at_]) + nn(wu_p[rows, :], gpr[U:, at_])
            pf[c, rows] = p
            for h in range(TC // 128):
                term = gb[rows, :] * p[:, h * 128 : (h + 1) * 128]
                acc[h] = acc[h] + jnp.sum(term.reshape(4 * W // 8, 8, 128), axis=0)
        for h in range(TC // 128):
            bst[0:1, pl.ds(c * TC + h * 128, 128)] = jnp.sum(acc[h], axis=0, keepdims=True)
        for d in range(2):
            s1[d, c] = pf[c, y_rows(anti, d * 2 * W, 2 * W)].astype(BF)
            go_out(rs1(c, d))

    cotangent(0)
    cotangent(1)
    gather_2(1, 0)
    gather_1(1, 2)
    gather_3(0, 3)
    cotangent(2)
    gather_2(1, 1)
    gather_3(1, 0)
    gather_1(1, 3)
    cotangent(3)
    gather_3(1, 1)
    gather_end(1, 0)
    layers(0, 0)
    gather_2(1, 2)
    layers(0, 1)
    gather_3(1, 2)
    back(0)
    gather_end(1, 1)
    layers(1, 0)
    gather_2(1, 3)
    layers(1, 1)
    gather_3(1, 3)
    back(1)
    rs2_step(0)
    gather_end(1, 2)
    layers(2, 0)
    layers(2, 1)
    back(2)
    rs2_step(1)
    gather_end(1, 3)
    layers(3, 0)
    rs3_step(0)
    layers(3, 1)

    order = (4, 3, 5, 2, 6, 1, 7, 0)

    def place(i):
        return lax.rem(z + order[i], NZ)

    def weight_blocks(first, count, which=(1, 0)):
        for a in which:
            left, right = ((g_n, gpr), (g_s, hid))[a]
            wide = []
            for c in range(NC):
                pieces = []
                for i in range(first, first + count):
                    for e in range(2):
                        pieces.append(left[c, rows_at(e * (NZ * W) + place(i) * W, W), :])
                wide.append(jnp.concatenate(pieces, axis=0))
            lhs = jnp.concatenate(wide, axis=1)
            theirs = nt(lhs, right[U:, :])
            for j in range(2 * count):
                c_s[first + j // 2, a, j % 2] = theirs[j * W : (j + 1) * W].astype(BF)
            for i in range(first, first + count):
                go_out(core_w(i, a))
            mine = nt(lhs, right[0:U, :])
            for j in range(2 * count):
                wf[first + j // 2, a, j % 2] = mine[j * W : (j + 1) * W]

    def both_cores(i, a, e):
        return wf[i, a, e] + c_r[i, a, e].astype(F32)

    def over_x(i):
        core_w(i, 1).wait_recv()
        e_s[i] = both_cores(i, 1, 1 - xl).astype(BF)
        go_out(x_early(i))

    def way(i):
        off = order[i]
        return (0, 4 - off) if off < 4 else (1, off - 4)

    def ring_up(i):
        core_w(i, 0).wait_recv()
        if order[i] == 4:
            for d in range(2):
                z_s[d, 0, d] = both_cores(i, 0, d).astype(BF)
                go_out(ring(d, 0, d))
        elif order[i] != 0:
            d, step = way(i)
            for e in (d, 1 - d):
                got = both_cores(i, 0, e)
                if step > 1 or e == d:
                    ring(d, step - 1, e).wait_recv()
                    got = got + z_r[d, step - 1, e].astype(F32)
                z_s[d, step, e] = got.astype(BF)
                go_out(ring(d, step, e))
        else:
            for e in range(2):
                for d in range(2):
                    ring(d, 3, e).wait_recv()

            def part(e):
                return both_cores(i, 0, e) + z_r[0, 3, e].astype(F32) + z_r[1, 3, e].astype(F32)

            x_s[...] = part(1 - xl).astype(BF)
            go_out(x_late())
            gu[...] = part(xl)

    def ring_down(i):
        x_early(i).wait_recv()
        mine = both_cores(i, 1, xl) + e_r[i].astype(F32)
        halves = (slice(0, W // 2), slice(W // 2, W))
        if order[i] == 4:
            for d, half in enumerate(halves):
                z_s[d, 0, 2, half] = mine[half].astype(BF)
                go_out(ring(d, 0, 2))
        elif order[i] != 0:
            d, step = way(i)
            ring(d, step - 1, 2).wait_recv()
            if step == 1:
                half, rest = halves[d], halves[1 - d]
                z_s[d, 1, 2, half] = (mine[half] + z_r[d, 0, 2, half].astype(F32)).astype(BF)
                z_s[d, 1, 2, rest] = mine[rest].astype(BF)
            else:
                z_s[d, step, 2] = (mine + z_r[d, step - 1, 2].astype(F32)).astype(BF)
            go_out(ring(d, step, 2))
        else:
            for d in range(2):
                ring(d, 3, 2).wait_recv()
            gd[...] = factor * (mine + z_r[0, 3, 2].astype(F32) + z_r[1, 3, 2].astype(F32))

    factor = 1.0 / math.sqrt(TOK * SEQ)
    weight_blocks(0, 1, (0, 1))
    ring_up(0)
    over_x(0)
    back(3)
    for j in range(3):
        go_out(bstat(0, j))
    rs2_step(2)
    weight_blocks(1, 2)
    ring_down(0)
    over_x(1)
    over_x(2)
    rs2_step(3)
    ring_up(1)
    ring_up(2)
    rs3_step(1)
    for j in range(3):
        bstat(0, j).wait_recv()
    b_m[...] = (bst[...] + b_1[2]) + (b_1[0] + b_1[1])
    for j in range(3):
        go_out(bstat(1, j))
    weight_blocks(3, 2)
    ring_down(1)
    ring_down(2)
    over_x(3)
    over_x(4)
    rs3_step(2)
    ring_up(3)
    ring_up(4)
    rs3_step(3)
    weight_blocks(5, 2)
    ring_down(3)
    ring_down(4)
    over_x(5)
    over_x(6)

    def norm_back(c):
        rel = pl.ds(c * TC, TC)
        for j in range(3):
            rs3(c, j).wait_recv()
        here = own[c] + r3[c, 0].astype(F32)
        there = r3[c, 1].astype(F32) + r3[c, 2].astype(F32)
        sums_here = (b_m[:, rel] + b_2[0, :, rel]) / D
        sums_there = (b_2[1, :, rel] + b_2[2, :, rel]) / D
        for h in range(2):
            at_ = pl.ds(h * HALF + c * TC, TC)
            sums = jnp.where(k == h, sums_here, sums_there)
            scaled_g = jnp.where(k == h, here, there) * gain_col
            rstd = mr[1:2, at_]
            nhat = (cv[:, at_] - mr[0:1, at_]) * rstd
            grad = rstd * (scaled_g - sums[0:1] - nhat * sums[1:2])
            gc[pl.ds(EDGE + h * HALF + c * TC, TC), :] = grad.T

    def tap_rows(i, sums):
        g = gc[pl.ds(pl.multiple_of(EDGE + i * ROWS, 8), ROWS), :]
        out = []
        for tap in range(KW):
            prod = g * xp[pl.ds(i * ROWS + tap + 1, ROWS), :]
            out.append(sums[tap] + jnp.sum(prod.reshape(ROWS // 8, 8, W), axis=0))
        return tuple(out)

    def back_rows(i, carry):
        at_ = pl.ds(pl.multiple_of(i * ROWS, ROWS), ROWS)
        total = None
        for tap in range(KW):
            term = taps[tap : tap + 1, :] * gc[pl.ds(i * ROWS + KW - tap, ROWS), :]
            total = term if total is None else total + term
        gi_t[:, at_] = (go_t[:, at_].astype(F32) + total.T).astype(BF)
        return carry

    for j in range(3):
        bstat(1, j).wait_recv()
    for c in range(NC - 1):
        norm_back(c)
    half_steps, early = steps // 2, (NC - 1) * TC // ROWS
    sums = (jnp.zeros((8, W), F32),) * KW
    for h in range(2):
        sums = lax.fori_loop(h * half_steps, h * half_steps + early, tap_rows, sums)
    norm_back(NC - 1)
    for d in range(2):
        go_out(ghalo(d))
    for h in range(2):
        sums = lax.fori_loop(h * half_steps + early, (h + 1) * half_steps, tap_rows, sums)
    for tap in range(KW):
        gks[tap : tap + 1, :] = jnp.sum(sums[tap], axis=0, keepdims=True)
    gks[KW : KW + 1, :] = jnp.zeros((1, W), F32)
    go_out(gk_x())
    ring_up(5)
    ring_up(6)
    weight_blocks(7, 1)
    ring_down(5)
    ring_down(6)
    gk_x().wait_recv()
    gk_m[...] = gks[...] + gk_1[...]
    for j in range(1, NZ):
        go_out(gk_z(j))
    over_x(7)
    lax.fori_loop(1, steps - 1, back_rows, 0)
    ring_up(7)
    for d in range(2):
        ghalo(d).wait_recv()
    gc[0:EDGE, :] = jnp.where(sq == 0, 0.0, gch[0])
    gc[pl.ds(EDGE + TOK, EDGE), :] = jnp.where(sq == SEQ - 1, 0.0, gch[1])
    back_rows(0, 0)
    back_rows(steps - 1, 0)
    total = gk_m[...]
    for j in range(1, NZ):
        gk_z(j).wait_recv()
        total = total + gk_2[j]
    gk[...] = total[0:KW] * factor
    ring_down(7)
    x_late().wait_recv()
    gu[...] = (gu[...] + x_r[...].astype(F32)) * factor

    for copy in sent:
        copy.wait_send()


def hand_on(*arrays):
    def copy_all(*refs):
        n = len(arrays)
        for src, dst in zip(refs[:n], refs[n:]):
            dst[...] = src[...]

    spec = pl.BlockSpec(memory_space=pltpu.VMEM)
    return pl.pallas_call(
        copy_all,
        out_shape=[jax.ShapeDtypeStruct(a.shape, a.dtype) for a in arrays],
        in_specs=[spec] * len(arrays),
        out_specs=[spec] * len(arrays),
    )(*arrays)


def block(inputs, grad_out, kernel, ln_gain, layer_scale, w_up, w_down):
    dma, vmem = pltpu.SemaphoreType.DMA, pltpu.VMEM
    scratch = [
        vmem((2, NC, W, TC), BF),
        vmem((2, NC, W, TC), BF),
        vmem((NC, D, TC), BF),
        vmem((NC, D, TC), BF),
        vmem((TOK + 2 * EDGE, W), F32),
        vmem((W, TOK), F32),
        vmem((2, 16, W), BF),
        vmem((2, 16, W), BF),
        vmem((2, TOK), F32),
        vmem((3, 2, TOK), F32),
        vmem((2, TOK), F32),
        vmem((3, 2, TOK), F32),
        vmem((2, TOK), F32),
        vmem((W, 128), F32),
        vmem((D, 128), F32),
        vmem((D, U), BF),
        vmem((U, D), BF),
        vmem((U, D), BF),
        vmem((D, U), BF),
        vmem((U, D), BF),
        vmem((U, D), BF),
        vmem((U, TC), F32),
        vmem((2 * U, HALF), BF),
        vmem((2 * U, HALF), BF),
        vmem((NC, D, TC), F32),
        vmem((2, NC, 2 * W, TC), BF),
        vmem((2, NC, 2 * W, TC), BF),
        vmem((2, NC, 4 * W, TC), BF),
        vmem((2, NC, 4 * W, TC), BF),
        vmem((NC, 3, W, TC), BF),
        vmem((NC, 3, W, TC), BF),
        vmem((NC, W, TC), F32),
        vmem((2, HALF), F32),
        vmem((3, 2, HALF), F32),
        vmem((2, HALF), F32),
        vmem((3, 2, HALF), F32),
        vmem((TOK + 2 * EDGE, W), F32),
        vmem((2, EDGE, W), F32),
        vmem((16, W), F32),
        vmem((16, W), F32),
        vmem((16, W), F32),
        vmem((NZ, 16, W), F32),
        vmem((NZ, 2, 2, W, U), F32),
        vmem((NZ, 2, 2, W, U), BF),
        vmem((NZ, 2, 2, W, U), BF),
        vmem((2, 4, 3, W, U), BF),
        vmem((2, 4, 3, W, U), BF),
        vmem((W, U), BF),
        vmem((W, U), BF),
        vmem((NZ, W, U), BF),
        vmem((NZ, W, U), BF),
    ]
    for count in (2, 3, 6, 24 * NC, 2 * NC, 2 * NC, 3 * NC, 6, 2, NZ, 2 * NZ, 24, 1, NZ, 2):
        scratch += [dma((count,)), dma((count,))]
    spec = pl.BlockSpec(memory_space=pltpu.VMEM)
    gi_t, gu, gd, gk = pl.pallas_call(
        body,
        out_shape=[
            jax.ShapeDtypeStruct((W, TOK), BF),
            jax.ShapeDtypeStruct((W, U), F32),
            jax.ShapeDtypeStruct((W, U), F32),
            jax.ShapeDtypeStruct((KW, W), F32),
        ],
        in_specs=[spec] * 5 + [pl.BlockSpec(memory_space=pl.ANY)] * 2,
        out_specs=[spec] * 4,
        scratch_shapes=scratch,
        compiler_params=pltpu.CompilerParams(
            collective_id=0, has_side_effects=True, vmem_limit_bytes=60 * 2**20
        ),
    )(inputs.T, grad_out.T, kernel, ln_gain, layer_scale, w_up, w_down)
    gi_t, gu, gd, gk = hand_on(gi_t, gu, gd, gk)
    return gi_t.T, gu, gd, gk


def solution(mesh):
    in_specs = (
        P("seq", "tp"),
        P("seq", "tp"),
        P(None, "tp"),
        P(),
        P(),
        P(None, "tp"),
        P("tp", None),
    )
    out_specs = (P("seq", "tp"), P("seq", "tp"), P("seq", "tp"), P(None, "tp"))
    return jax.shard_map(block, mesh=mesh, in_specs=in_specs, out_specs=out_specs, check_vma=False)
```

```python
import math

import jax
import jax.numpy as jnp
from jax import lax
from jax.experimental import pallas as pl
from jax.experimental.pallas import tpu as pltpu
from jax.sharding import PartitionSpec as P

MESH = pl.DeviceIdType.MESH
BF = jnp.bfloat16
F32 = jnp.float32

TP = 16
NY = 4
SEQ = 16
NZ = 8
W = 96
D = 1536
TOK = 2048
HALF = TOK // 2
NC = 4
TC = HALF // NC
U = 384
KW = 15
EDGE = 8
ROWS = 128

X_FIRST = ((False, True, False, True), (False, True, True, True))


def nn(a, b):
    return jnp.dot(a, b, preferred_element_type=F32)


def nt(a, b):
    return lax.dot_general(a, b, (((1,), (1,)), ((), ())), preferred_element_type=F32)


def body(
    x_t, go_t, taps, gain, scale, wu_hbm, wd_hbm,
    gi_t, gu, gd, gk,
    s_st, n_st, g_s, g_n, xp, cv, h_st, hin, st_s, st_1, st_m, st_2, mr, cols, gb, wu, wd, wu_t, wu_p, wu_tp,
    wd_p, pre_s, hid, gpr, pf, s1, r1, s2, r2, s3, r3, own, bst, b_1, b_m, b_2, gc, gch,
    gks, gk_1, gk_m, gk_2, wf, c_s, c_r, z_s, z_r, x_s, x_r, e_s, e_r,
    halo_ss, halo_rs, w_ss, w_rs, st_ss, st_rs, ag_ss, ag_rs,
    r1_ss, r1_rs, r2_ss, r2_rs, r3_ss, r3_rs, b_ss, b_rs, gh_ss, gh_rs, gk_ss, gk_rs,
    c_ss, c_rs, z_ss, z_rs, x_ss, x_rs, e_ss, e_rs, in_ss, _,
):
    tp = lax.axis_index("tp")
    sq = lax.axis_index("seq")
    k = lax.rem(tp, 2)
    xh = lax.rem(tp // 2, 2)
    y = tp // 4
    xl = sq // NZ
    z = lax.rem(sq, NZ)
    sent = []

    def at(y_, xh_, k_):
        return {"seq": sq, "tp": (y_ * 2 + xh_) * 2 + k_}

    def send(src, dst, ss, rs, dev):
        return pltpu.make_async_remote_copy(
            src_ref=src, dst_ref=dst, send_sem=ss, recv_sem=rs, device_id=dev, device_id_type=MESH
        )

    def go_out(copy):
        copy.start()
        sent.append(copy)

    up, down = lax.rem(y + 1, NY), lax.rem(y + NY - 1, NY)
    anti = lax.rem(y + 2, NY)
    y_dev = (at(up, xh, k), at(down, xh, k), at(anti, xh, k))
    other = 1 - k
    near = (at(y, 1 - xh, k), at(y, xh, other), at(y, 1 - xh, other))
    sq_next, sq_prev = lax.rem(sq + 1, SEQ), lax.rem(sq + SEQ - 1, SEQ)
    sq_dev = ({"seq": sq_next, "tp": tp}, {"seq": sq_prev, "tp": tp})
    z_dev = [{"seq": xl * NZ + lax.rem(z + j, NZ), "tp": tp} for j in range(NZ)]
    z_ring = (z_dev[1], z_dev[NZ - 1])
    x_dev = {"seq": (1 - xl) * NZ + z, "tp": tp}

    def rows_at(first, count):
        return pl.ds(pl.multiple_of(first, 32), count)

    def y_rows(which, first=0, count=4 * W):
        return rows_at(which * (4 * W) + first, count)

    def pair_rows(which, first=0, count=2 * W):
        return rows_at(which * (4 * W) + xh * (2 * W) + first, count)

    my_rows = rows_at(tp * W, W)

    barrier = pltpu.get_barrier_semaphore()
    partners = [*near, *y_dev, *sq_dev, *z_dev[1:], x_dev]
    weights_in = (
        pltpu.make_async_copy(wu_hbm, wu, in_ss.at[0]),
        pltpu.make_async_copy(wd_hbm, wd, in_ss.at[1]),
    )
    for dev in partners:
        pl.semaphore_signal(barrier, inc=1, device_id=dev, device_id_type=MESH)

    for copy in weights_in:
        copy.start()

    def halo(d):
        return send(h_st.at[d], hin.at[d], halo_ss.at[d], halo_rs.at[d], sq_dev[d])

    def weight(i):
        src, dst = ((wd, wd_p), (wu, wu_p), (wu_t, wu_tp))[i]
        return send(src, dst, w_ss.at[i], w_rs.at[i], near[1])

    def stat(stage, j):
        src, dst, dev = ((st_s, st_1, near), (st_m, st_2, y_dev))[stage]
        i = stage * 3 + j
        return send(src, dst.at[j], st_ss.at[i], st_rs.at[i], dev[j])

    def bstat(stage, j):
        src, dst, dev = ((bst, b_1, y_dev), (b_m, b_2, near))[stage]
        i = stage * 3 + j
        return send(src, dst.at[j], b_ss.at[i], b_rs.at[i], dev[j])

    staged, full = (s_st, n_st), (g_s, g_n)

    def gather(a, c, slot):
        i = (a * NC + c) * 10 + slot
        buf = full[a].at[c]
        if slot < 3:
            src = staged[a].at[k if slot == 0 else other, c]
            return send(src, buf.at[my_rows], ag_ss.at[i], ag_rs.at[i], near[slot])
        if X_FIRST[a][c]:
            part, dev = (
                (y_rows(y), y_dev[0]),
                (y_rows(y), y_dev[1]),
                (y_rows(down, 0, 2 * W), y_dev[0]),
                (y_rows(up, 2 * W, 2 * W), y_dev[1]),
            )[slot - 3]
        else:
            part, dev = (
                (pair_rows(y), y_dev[0]),
                (pair_rows(y), y_dev[1]),
                (pair_rows(down, 0, W), y_dev[0]),
                (pair_rows(up, W, W), y_dev[1]),
                (pair_rows(y), near[0]),
                (pair_rows(down), near[0]),
                (pair_rows(up), near[0]),
            )[slot - 3]
        part = buf.at[part]
        return send(part, part, ag_ss.at[i], ag_rs.at[i], dev)

    def gather_last(a, c, d):
        i = (a * NC + c) * 2 + d
        part = full[a].at[c].at[pair_rows(anti, d * W, W)]
        i = 2 * NC * 10 + i
        return send(part, part, ag_ss.at[i], ag_rs.at[i], near[0])

    def gather_0(a, c):
        for slot in (2, 0, 1) if X_FIRST[a][c] else (1,):
            go_out(gather(a, c, slot))
        full[a][c, my_rows] = staged[a][k, c]

    def gather_1(a, c):
        for slot in (2, 0, 1) if X_FIRST[a][c] else (1,):
            gather(a, c, slot).wait_recv()
        go_out(gather(a, c, 3))
        go_out(gather(a, c, 4))
        if not X_FIRST[a][c]:
            go_out(gather(a, c, 7))

    def gather_2(a, c):
        for d in range(2):
            gather(a, c, 3 + d).wait_recv()
            go_out(gather(a, c, 5 + d))
            if not X_FIRST[a][c]:
                go_out(gather(a, c, 8 + d))

    def gather_3(a, c):
        if not X_FIRST[a][c]:
            for d in range(2):
                gather(a, c, 5 + d).wait_recv()
                go_out(gather_last(a, c, d))

    def gather_end(a, c):
        if X_FIRST[a][c]:
            for d in range(2):
                gather(a, c, 5 + d).wait_recv()
        else:
            for slot in (7, 8, 9):
                gather(a, c, slot).wait_recv()
            for d in range(2):
                gather_last(a, c, d).wait_recv()

    def rs1(c, d):
        i = c * 2 + d
        return send(s1.at[d, c], r1.at[d, c], r1_ss.at[i], r1_rs.at[i], y_dev[d])

    def rs2(c, d):
        i = c * 2 + d
        return send(s2.at[d, c], r2.at[d, c], r2_ss.at[i], r2_rs.at[i], y_dev[d])

    def rs3(c, j):
        i = c * 3 + j
        return send(s3.at[c, j], r3.at[c, j], r3_ss.at[i], r3_rs.at[i], near[j])

    def ghalo(d):
        src = gc.at[pl.ds(TOK, EDGE)] if d == 0 else gc.at[pl.ds(EDGE, EDGE)]
        return send(src, gch.at[d], gh_ss.at[d], gh_rs.at[d], sq_dev[d])

    def gk_x():
        return send(gks, gk_1, gk_ss.at[0], gk_rs.at[0], x_dev)

    def gk_z(j):
        return send(gk_m, gk_2.at[j], gk_ss.at[j], gk_rs.at[j], z_dev[j])

    def core_w(i, a):
        j = i * 2 + a
        return send(c_s.at[i, a], c_r.at[i, a], c_ss.at[j], c_rs.at[j], near[1])

    def ring(d, step, p):
        i = (d * 4 + step) * 3 + p
        src, dst = z_s.at[d, step, p], z_r.at[d, step, p]
        if step == 0 and p == 2:
            half = pl.ds(d * (W // 2), W // 2)
            src, dst = src.at[half], dst.at[half]
        return send(src, dst, z_ss.at[i], z_rs.at[i], z_ring[d])

    def x_early(i):
        return send(e_s.at[i], e_r.at[i], e_ss.at[i], e_rs.at[i], x_dev)

    def x_late():
        return send(x_s, x_r, x_ss.at[0], x_rs.at[0], x_dev)

    turn = lax.rem(D - tp * W, D)

    def local_column(ref):
        row = pltpu.roll(jnp.broadcast_to(ref[...].reshape(1, D), (8, D)), turn, 1)[0:1, 0:128]
        return jnp.broadcast_to(row, (128, 128)).T[0:W, 0:1]

    scale_col = local_column(scale)
    for c in range(NC):
        for h in range(2):
            at_ = pl.ds(h * HALF + c * TC, TC)
            s_st[h, c] = (scale_col * go_t[:, at_].astype(F32)).astype(BF)
    h_st[0] = x_t[:, pl.ds(TOK - 128, 128)].astype(F32).T[112:128].astype(BF)
    h_st[1] = x_t[:, pl.ds(0, 128)].astype(F32).T[0:16].astype(BF)
    cols[...] = jnp.broadcast_to(local_column(gain), (W, 128))

    def load(i, carry):
        block_t = x_t[:, pl.ds(pl.multiple_of(i * ROWS, ROWS), ROWS)].astype(F32)
        xp[pl.ds(pl.multiple_of(EDGE + i * ROWS, 8), ROWS), :] = block_t.T
        return carry

    steps = TOK // ROWS
    lax.fori_loop(0, steps, load, 0)
    pl.semaphore_wait(barrier, len(partners))
    for d in range(2):
        go_out(halo(d))
    for c in range(NC):
        gather_0(0, c)
    def conv_rows(i, carry):
        total = None
        for tap in range(KW):
            term = taps[tap : tap + 1, :] * xp[pl.ds(i * ROWS + tap + 1, ROWS), :]
            total = term if total is None else total + term
        out = total.T
        at_ = pl.ds(pl.multiple_of(i * ROWS, ROWS), ROWS)
        cv[:, at_] = out
        st_s[0:1, at_] = jnp.sum(out, axis=0, keepdims=True)
        st_s[1:2, at_] = jnp.sum(out * out, axis=0, keepdims=True)
        return carry

    lax.fori_loop(1, steps // 2, conv_rows, 0)
    gather_1(0, 0)
    for d in range(2):
        halo(d).wait_recv()
    xp[0:EDGE, :] = jnp.where(sq == 0, 0.0, hin[0].astype(F32)[8:16])
    xp[pl.ds(EDGE + TOK, EDGE), :] = jnp.where(sq == SEQ - 1, 0.0, hin[1].astype(F32)[0:8])
    gather_1(0, 1)
    conv_rows(0, 0)
    lax.fori_loop(steps // 2, steps, conv_rows, 0)
    for j in range(3):
        go_out(stat(0, j))
    gather_1(0, 2)
    gather_2(0, 0)
    gather_1(0, 3)
    for j in range(3):
        stat(0, j).wait_recv()
    st_m[...] = (st_s[...] + st_1[1]) + (st_1[0] + st_1[2])
    for j in range(3):
        go_out(stat(1, j))
    for copy in weights_in:
        copy.wait()
    for i in range(2):
        go_out(weight(i))
    gather_3(0, 0)

    for i in range(D // 128):
        part = slice(i * 128, (i + 1) * 128)
        wu_t[:, part] = wu[part, :].T
        gb[part, :] = jnp.broadcast_to(gain[part].reshape(1, 128), (128, 128)).T
    go_out(weight(2))

    for j in range(3):
        stat(1, j).wait_recv()
    totals = (st_m[...] + st_2[2]) + (st_2[0] + st_2[1])
    mean = totals[0:1] / D
    var = totals[1:2] / D - mean * mean
    mr[0:1, :] = mean
    mr[1:2, :] = lax.rsqrt(var + 1e-06)
    gain_col = cols[:, 0:1]
    for c in range(NC):
        for h in range(2):
            at_ = pl.ds(h * HALF + c * TC, TC)
            nhat = (cv[:, at_] - mr[0:1, at_]) * mr[1:2, at_]
            n_st[h, c] = (nhat * gain_col).astype(BF)
        gather_0(1, c)
    gather_2(0, 1)
    gather_1(1, 0)
    gather_2(0, 2)
    gather_3(0, 1)
    gather_1(1, 1)
    gather_2(0, 3)
    gather_3(0, 2)
    for i in range(3):
        weight(i).wait_recv()

    def cotangent(c):
        gather_end(0, c)
        pf[c, 0:U] = nn(wd[...], g_s[c])
        pf[c, U : 2 * U] = nn(wd_p[...], g_s[c])

    def rs2_step(c):
        for d, to in ((0, up), (1, down)):
            rs1(c, d).wait_recv()
            a, b = d * 2 * W, (1 - d) * 2 * W
            got = pf[c, y_rows(to, a, 2 * W)] + r1[d, c].astype(F32)
            s2[d, c, pl.ds(a, 2 * W)] = got.astype(BF)
            s2[d, c, pl.ds(b, 2 * W)] = pf[c, y_rows(to, b, 2 * W)].astype(BF)
            go_out(rs2(c, d))

    def rs3_step(c):
        for d in range(2):
            rs2(c, d).wait_recv()

        def group(g):
            rows = rows_at(g * W, W)
            mine = pf[c, y_rows(y, g * W, W)]
            return mine + r2[0, c, rows].astype(F32) + r2[1, c, rows].astype(F32)

        for j, (xh_, k_) in ((2, (1 - xh, other)), (0, (1 - xh, k)), (1, (xh, other))):
            s3[c, j] = group(xh_ * 2 + k_).astype(BF)
            go_out(rs3(c, j))
        own[c] = group(xh * 2 + k)

    def layers(c, u):
        at_ = pl.ds(c * TC, TC)
        pre_s[...] = nn((wu_t, wu_tp)[u][...], g_n[c])

        def act(i, acc):
            v = pre_s[rows_at(i * 32, 32), :]
            to = rows_at(u * U + i * 32, 32)
            phi = 0.5 + 0.5 * lax.erf(v * 0.7071067811865476)
            slope = phi + v * jnp.exp(-0.5 * v * v) * 0.3989422804014327
            gp = (pf[c, to] * slope).astype(BF)
            hid[to, at_] = (v * phi).astype(BF)
            gpr[to, at_] = gp
            return acc + jnp.sum((gp.astype(F32) * v).reshape(4, 8, TC), axis=0)

        acc = lax.fori_loop(0, U // 32, act, jnp.zeros((8, TC), F32))
        total = jnp.sum(acc, axis=0, keepdims=True)
        bst[1:2, at_] = total if u == 0 else bst[1:2, at_] + total

    def back(c):
        at_ = pl.ds(c * TC, TC)
        acc = [jnp.zeros((8, 128), F32)] * (TC // 128)
        for r in range(NY):
            rows = pl.ds(r * 4 * W, 4 * W)
            p = nn(wu[rows, :], gpr[0:U, at_]) + nn(wu_p[rows, :], gpr[U:, at_])
            pf[c, rows] = p
            for h in range(TC // 128):
                term = gb[rows, :] * p[:, h * 128 : (h + 1) * 128]
                acc[h] = acc[h] + jnp.sum(term.reshape(4 * W // 8, 8, 128), axis=0)
        for h in range(TC // 128):
            bst[0:1, pl.ds(c * TC + h * 128, 128)] = jnp.sum(acc[h], axis=0, keepdims=True)
        for d in range(2):
            s1[d, c] = pf[c, y_rows(anti, d * 2 * W, 2 * W)].astype(BF)
            go_out(rs1(c, d))

    cotangent(0)
    cotangent(1)
    gather_2(1, 0)
    gather_1(1, 2)
    gather_3(0, 3)
    cotangent(2)
    gather_2(1, 1)
    gather_3(1, 0)
    gather_1(1, 3)
    cotangent(3)
    gather_3(1, 1)
    gather_end(1, 0)
    layers(0, 0)
    gather_2(1, 2)
    layers(0, 1)
    gather_3(1, 2)
    back(0)
    gather_end(1, 1)
    layers(1, 0)
    gather_2(1, 3)
    layers(1, 1)
    gather_3(1, 3)
    back(1)
    rs2_step(0)
    gather_end(1, 2)
    layers(2, 0)
    layers(2, 1)
    back(2)
    gather_end(1, 3)
    rs2_step(1)
    layers(3, 0)
    rs3_step(0)
    layers(3, 1)

    order = (4, 3, 5, 2, 6, 1, 7, 0)

    def place(i):
        return lax.rem(z + order[i], NZ)

    def weight_blocks(first, count, which=(1, 0)):
        for a in which:
            left, right = ((g_n, gpr), (g_s, hid))[a]
            wide = []
            for c in range(NC):
                pieces = []
                for i in range(first, first + count):
                    for e in range(2):
                        pieces.append(left[c, rows_at(e * (NZ * W) + place(i) * W, W), :])
                wide.append(jnp.concatenate(pieces, axis=0))
            lhs = jnp.concatenate(wide, axis=1)
            theirs = nt(lhs, right[U:, :])
            for j in range(2 * count):
                c_s[first + j // 2, a, j % 2] = theirs[j * W : (j + 1) * W].astype(BF)
            for i in range(first, first + count):
                go_out(core_w(i, a))
            mine = nt(lhs, right[0:U, :])
            for j in range(2 * count):
                wf[first + j // 2, a, j % 2] = mine[j * W : (j + 1) * W]

    def both_cores(i, a, e):
        return wf[i, a, e] + c_r[i, a, e].astype(F32)

    def over_x(i):
        core_w(i, 1).wait_recv()
        e_s[i] = both_cores(i, 1, 1 - xl).astype(BF)
        go_out(x_early(i))

    def way(i):
        off = order[i]
        return (0, 4 - off) if off < 4 else (1, off - 4)

    def ring_up(i):
        core_w(i, 0).wait_recv()
        if order[i] == 4:
            for d in range(2):
                z_s[d, 0, d] = both_cores(i, 0, d).astype(BF)
                go_out(ring(d, 0, d))
        elif order[i] != 0:
            d, step = way(i)
            for e in (d, 1 - d):
                got = both_cores(i, 0, e)
                if step > 1 or e == d:
                    ring(d, step - 1, e).wait_recv()
                    got = got + z_r[d, step - 1, e].astype(F32)
                z_s[d, step, e] = got.astype(BF)
                go_out(ring(d, step, e))
        else:
            for e in range(2):
                for d in range(2):
                    ring(d, 3, e).wait_recv()

            def part(e):
                return both_cores(i, 0, e) + z_r[0, 3, e].astype(F32) + z_r[1, 3, e].astype(F32)

            x_s[...] = part(1 - xl).astype(BF)
            go_out(x_late())
            gu[...] = part(xl)

    def ring_down(i):
        x_early(i).wait_recv()
        mine = both_cores(i, 1, xl) + e_r[i].astype(F32)
        halves = (slice(0, W // 2), slice(W // 2, W))
        if order[i] == 4:
            for d, half in enumerate(halves):
                z_s[d, 0, 2, half] = mine[half].astype(BF)
                go_out(ring(d, 0, 2))
        elif order[i] != 0:
            d, step = way(i)
            ring(d, step - 1, 2).wait_recv()
            if step == 1:
                half, rest = halves[d], halves[1 - d]
                z_s[d, 1, 2, half] = (mine[half] + z_r[d, 0, 2, half].astype(F32)).astype(BF)
                z_s[d, 1, 2, rest] = mine[rest].astype(BF)
            else:
                z_s[d, step, 2] = (mine + z_r[d, step - 1, 2].astype(F32)).astype(BF)
            go_out(ring(d, step, 2))
        else:
            for d in range(2):
                ring(d, 3, 2).wait_recv()
            gd[...] = factor * (mine + z_r[0, 3, 2].astype(F32) + z_r[1, 3, 2].astype(F32))

    factor = 1.0 / math.sqrt(TOK * SEQ)
    weight_blocks(0, 1, (0, 1))
    ring_up(0)
    over_x(0)
    back(3)
    for j in range(3):
        go_out(bstat(0, j))
    rs2_step(2)
    weight_blocks(1, 2)
    ring_down(0)
    over_x(1)
    over_x(2)
    rs2_step(3)
    ring_up(1)
    ring_up(2)
    rs3_step(1)
    for j in range(3):
        bstat(0, j).wait_recv()
    b_m[...] = (bst[...] + b_1[2]) + (b_1[0] + b_1[1])
    for j in range(3):
        go_out(bstat(1, j))
    weight_blocks(3, 2)
    ring_down(1)
    ring_down(2)
    over_x(3)
    over_x(4)
    rs3_step(2)
    ring_up(3)
    ring_up(4)
    rs3_step(3)
    weight_blocks(5, 2)
    ring_down(3)
    ring_down(4)
    over_x(5)
    over_x(6)

    def norm_back(c):
        rel = pl.ds(c * TC, TC)
        for j in range(3):
            rs3(c, j).wait_recv()
        here = own[c] + r3[c, 0].astype(F32)
        there = r3[c, 1].astype(F32) + r3[c, 2].astype(F32)
        sums_here = (b_m[:, rel] + b_2[0, :, rel]) / D
        sums_there = (b_2[1, :, rel] + b_2[2, :, rel]) / D
        for h in range(2):
            at_ = pl.ds(h * HALF + c * TC, TC)
            sums = jnp.where(k == h, sums_here, sums_there)
            scaled_g = jnp.where(k == h, here, there) * gain_col
            rstd = mr[1:2, at_]
            nhat = (cv[:, at_] - mr[0:1, at_]) * rstd
            grad = rstd * (scaled_g - sums[0:1] - nhat * sums[1:2])
            gc[pl.ds(EDGE + h * HALF + c * TC, TC), :] = grad.T

    def tap_rows(i, sums):
        g = gc[pl.ds(pl.multiple_of(EDGE + i * ROWS, 8), ROWS), :]
        out = []
        for tap in range(KW):
            prod = g * xp[pl.ds(i * ROWS + tap + 1, ROWS), :]
            out.append(sums[tap] + jnp.sum(prod.reshape(ROWS // 8, 8, W), axis=0))
        return tuple(out)

    def back_rows(i, carry):
        at_ = pl.ds(pl.multiple_of(i * ROWS, ROWS), ROWS)
        total = None
        for tap in range(KW):
            term = taps[tap : tap + 1, :] * gc[pl.ds(i * ROWS + KW - tap, ROWS), :]
            total = term if total is None else total + term
        gi_t[:, at_] = (go_t[:, at_].astype(F32) + total.T).astype(BF)
        return carry

    for j in range(3):
        bstat(1, j).wait_recv()
    for c in range(NC - 1):
        norm_back(c)
    half_steps, early = steps // 2, (NC - 1) * TC // ROWS
    sums = (jnp.zeros((8, W), F32),) * KW
    for h in range(2):
        sums = lax.fori_loop(h * half_steps, h * half_steps + early, tap_rows, sums)
    norm_back(NC - 1)
    for d in range(2):
        go_out(ghalo(d))
    for h in range(2):
        sums = lax.fori_loop(h * half_steps + early, (h + 1) * half_steps, tap_rows, sums)
    for tap in range(KW):
        gks[tap : tap + 1, :] = jnp.sum(sums[tap], axis=0, keepdims=True)
    gks[KW : KW + 1, :] = jnp.zeros((1, W), F32)
    go_out(gk_x())
    ring_up(5)
    ring_up(6)
    weight_blocks(7, 1)
    ring_down(5)
    ring_down(6)
    gk_x().wait_recv()
    gk_m[...] = gks[...] + gk_1[...]
    for j in range(1, NZ):
        go_out(gk_z(j))
    over_x(7)
    lax.fori_loop(1, steps - 1, back_rows, 0)
    ring_up(7)
    for d in range(2):
        ghalo(d).wait_recv()
    gc[0:EDGE, :] = jnp.where(sq == 0, 0.0, gch[0])
    gc[pl.ds(EDGE + TOK, EDGE), :] = jnp.where(sq == SEQ - 1, 0.0, gch[1])
    back_rows(0, 0)
    back_rows(steps - 1, 0)
    total = gk_m[...]
    for j in range(1, NZ):
        gk_z(j).wait_recv()
        total = total + gk_2[j]
    gk[...] = total[0:KW] * factor
    ring_down(7)
    x_late().wait_recv()
    gu[...] = (gu[...] + x_r[...].astype(F32)) * factor

    for copy in sent:
        copy.wait_send()


def hand_on(*arrays):
    n = len(arrays)

    def copy_all(*refs):
        srcs, dsts, held, sem = refs[:n], refs[n : 2 * n], refs[2 * n : 3 * n], refs[3 * n]
        into = [pltpu.make_async_copy(srcs[i], held[i], sem.at[i]) for i in range(n)]
        out = [pltpu.make_async_copy(held[i], dsts[i], sem.at[n + i]) for i in range(n)]
        for copy in into:
            copy.start()
        for i in range(n):
            into[i].wait()
            out[i].start()
        for copy in out:
            copy.wait()

    spec = pl.BlockSpec(memory_space=pl.ANY)
    return pl.pallas_call(
        copy_all,
        out_shape=[jax.ShapeDtypeStruct(a.shape, a.dtype) for a in arrays],
        in_specs=[spec] * n,
        out_specs=[spec] * n,
        scratch_shapes=[pltpu.VMEM(a.shape, a.dtype) for a in arrays]
        + [pltpu.SemaphoreType.DMA((2 * n,))],
    )(*arrays)


def block(inputs, grad_out, kernel, ln_gain, layer_scale, w_up, w_down):
    dma, vmem = pltpu.SemaphoreType.DMA, pltpu.VMEM
    scratch = [
        vmem((2, NC, W, TC), BF),
        vmem((2, NC, W, TC), BF),
        vmem((NC, D, TC), BF),
        vmem((NC, D, TC), BF),
        vmem((TOK + 2 * EDGE, W), F32),
        vmem((W, TOK), F32),
        vmem((2, 16, W), BF),
        vmem((2, 16, W), BF),
        vmem((2, TOK), F32),
        vmem((3, 2, TOK), F32),
        vmem((2, TOK), F32),
        vmem((3, 2, TOK), F32),
        vmem((2, TOK), F32),
        vmem((W, 128), F32),
        vmem((D, 128), F32),
        vmem((D, U), BF),
        vmem((U, D), BF),
        vmem((U, D), BF),
        vmem((D, U), BF),
        vmem((U, D), BF),
        vmem((U, D), BF),
        vmem((U, TC), F32),
        vmem((2 * U, HALF), BF),
        vmem((2 * U, HALF), BF),
        vmem((NC, D, TC), F32),
        vmem((2, NC, 2 * W, TC), BF),
        vmem((2, NC, 2 * W, TC), BF),
        vmem((2, NC, 4 * W, TC), BF),
        vmem((2, NC, 4 * W, TC), BF),
        vmem((NC, 3, W, TC), BF),
        vmem((NC, 3, W, TC), BF),
        vmem((NC, W, TC), F32),
        vmem((2, HALF), F32),
        vmem((3, 2, HALF), F32),
        vmem((2, HALF), F32),
        vmem((3, 2, HALF), F32),
        vmem((TOK + 2 * EDGE, W), F32),
        vmem((2, EDGE, W), F32),
        vmem((16, W), F32),
        vmem((16, W), F32),
        vmem((16, W), F32),
        vmem((NZ, 16, W), F32),
        vmem((NZ, 2, 2, W, U), F32),
        vmem((NZ, 2, 2, W, U), BF),
        vmem((NZ, 2, 2, W, U), BF),
        vmem((2, 4, 3, W, U), BF),
        vmem((2, 4, 3, W, U), BF),
        vmem((W, U), BF),
        vmem((W, U), BF),
        vmem((NZ, W, U), BF),
        vmem((NZ, W, U), BF),
    ]
    for count in (2, 3, 6, 24 * NC, 2 * NC, 2 * NC, 3 * NC, 6, 2, NZ, 2 * NZ, 24, 1, NZ, 2):
        scratch += [dma((count,)), dma((count,))]
    spec = pl.BlockSpec(memory_space=pltpu.VMEM)
    gi_t, gu, gd, gk = pl.pallas_call(
        body,
        out_shape=[
            jax.ShapeDtypeStruct((W, TOK), BF),
            jax.ShapeDtypeStruct((W, U), F32),
            jax.ShapeDtypeStruct((W, U), F32),
            jax.ShapeDtypeStruct((KW, W), F32),
        ],
        in_specs=[spec] * 5 + [pl.BlockSpec(memory_space=pl.ANY)] * 2,
        out_specs=[spec] * 4,
        scratch_shapes=scratch,
        compiler_params=pltpu.CompilerParams(
            collective_id=0, has_side_effects=True, vmem_limit_bytes=60 * 2**20
        ),
    )(inputs.T, grad_out.T, kernel, ln_gain, layer_scale, w_up, w_down)
    gi_t, gu, gd, gk = hand_on(gi_t, gu, gd, gk)
    return gi_t.T, gu, gd, gk


def solution(mesh):
    in_specs = (
        P("seq", "tp"),
        P("seq", "tp"),
        P(None, "tp"),
        P(),
        P(),
        P(None, "tp"),
        P("tp", None),
    )
    out_specs = (P("seq", "tp"), P("seq", "tp"), P("seq", "tp"), P(None, "tp"))
    return jax.shard_map(block, mesh=mesh, in_specs=in_specs, out_specs=out_specs, check_vma=False)
```
